512 devices in a mesh: col: 64 (over y, z_hi, core), feat: 8 (over x, z_lo).
Axes of the slice: x: 4, y: 8, z: 8 (z_hi: 4, z_lo: 2; z = z_hi * 2 + z_lo), core: 2. Of those that a mesh axis runs over, the one named last changes fastest.
Arguments:
- features_t: bfloat16 [128, 65536], P('feat', 'col'), may hold values from -6 to 6
- node_order: int32 [65536], P('col'), may hold values from 0 to 65535, as said below
- tile_rows: int32 [64, 96], P('col'), may hold values from 0 to 511, as said below
- tile_cols: int32 [64, 96], P('col'), may hold values from 0 to 7
- tile_vals: bfloat16 [64, 96, 128, 128], P('col'), may hold values from -0.21875 to 0.21875
- tile_count: int32 [64], P('col'), may hold values from 2 to 96, as said below
- weight: bfloat16 [128, 256], replicated, may hold values from -0.5 to 0.5
- bias_term: float32 [256], replicated, may hold values from -3 to 3
- cotangent: bfloat16 [256, 65536], P(None, ('col', 'feat')), may hold values from -6 to 6
Outputs:
- activated: bfloat16 [256, 65536], P(None, ('col', 'feat'))
- grad_weight: float32 [128, 256], replicated
- grad_bias: float32 [256], replicated
- grad_features: bfloat16 [128, 65536], P('feat', 'col')
The draws below stay inside these ranges and needn't reach their ends.
Inputs may be any that keep to these rules, and one draw needn't show every extreme that they name: `node_order`: A permutation of all nodes that maps the 1024 positions of each column group onto that group's own nodes of the input order. `tile_count`: slots at or after a group's count are not part of the adjacency. Some column group uses all 96 slots. Every count is 2 or more. `tile_rows`: slot s of column group g names the row block o * 8 + (g + q) mod 8 for an owning group o and some q from 0 to 1, so a group's slots name at most 2 row blocks of any one owner. In every group, slot s below 2 has o = g and q = s.
All inputs are finite; a program needn't handle non-finite values.
Results may differ from the reference program's by a relative error of at most 0.007.
Values may be sent and summed in bfloat16 or wider, within the bound.
A program may use at most 64 MiB of HBM per device.

```python
import jax
import jax.numpy as jnp
from jax import lax

F_IN = 128
HID = 256
BLOCK = 128
ROWCAP = 2
COLBLK = 8
TILES = 96
NODES_COL = 1024
NODES = 65536
BLOCKS = 512
N_COL = 64


def draw_tile_cols(key, part):
    key = jax.random.fold_in(key, 5)
    return jax.random.randint(key, (BLOCKS // COLBLK, TILES), 0, COLBLK).astype(jnp.int32)


def draw_tile_rows(key, part):
    key = jax.random.fold_in(key, 7)
    near_key, far_key, pick_key, within_key = jax.random.split(key, 4)
    group_total = BLOCKS // COLBLK
    home = jnp.arange(group_total, dtype=jnp.int32)[:, None]
    offset = jax.random.randint(near_key, (group_total, TILES), -2, 3)
    near = (home + offset + 4 * group_total) % group_total
    far = jax.random.randint(far_key, (group_total, TILES), 0, group_total)
    pick = jax.random.randint(pick_key, (group_total, TILES), 0, 2)
    owner = jnp.where(pick == 0, near, far)
    within = jax.random.randint(within_key, (group_total, TILES), 0, ROWCAP)
    slot_ids = jnp.arange(TILES, dtype=jnp.int32)[None, :]
    owner = jnp.where(slot_ids < ROWCAP, home, owner)
    within = jnp.where(slot_ids < ROWCAP, slot_ids, within)
    return (owner * COLBLK + (home + within) % COLBLK).astype(jnp.int32)


def draw_tile_count(key, part):
    key = jax.random.fold_in(key, 11)
    spread_key, full_key = jax.random.split(key)
    group_total = BLOCKS // COLBLK
    spread = jax.random.randint(spread_key, (group_total,), 0, TILES + 1)
    counts = TILES // 8 + (TILES - TILES // 8) * spread * spread // (TILES * TILES)
    chosen = jax.random.randint(full_key, (), 0, group_total)
    counts = jnp.where(jnp.arange(group_total) == chosen, TILES, counts)
    return jnp.maximum(counts, ROWCAP).astype(jnp.int32)


def draw_node_order(key, part):
    key = jax.random.fold_in(key, 13)
    group_total = NODES // NODES_COL
    group_keys = jax.random.split(key, group_total)
    inner = jax.vmap(lambda one_key: jax.random.permutation(one_key, NODES_COL))(group_keys)
    shifted = inner + jnp.arange(group_total, dtype=jnp.int32)[:, None] * NODES_COL
    return shifted.reshape(-1).astype(jnp.int32)


def block_scale(rng, extent, cuts, low, top_value):
    factor_of, own = 1.0, jax.random.fold_in(rng, 6)
    for axis_at, parts in cuts:
        draws = jnp.exp(jax.random.uniform(jax.random.fold_in(own, axis_at), (parts,), jnp.float32, low / len(cuts), top_value / len(cuts)))
        factor_of = factor_of * jnp.repeat(draws, extent[axis_at] // parts).reshape([-1 if axis == axis_at else 1 for axis in range(len(extent))])
    return factor_of


def bell_draw(stream_key, shape, width, bound, pieces=(), kind=jnp.bfloat16):
    loudness = block_scale(stream_key, shape, pieces, -0.22, 0.18) if pieces else 1.0
    result = jax.random.normal(stream_key, shape, jnp.float32) * width * loudness
    return jnp.minimum(jnp.maximum(result, -bound), bound).astype(kind)


def setup_inputs(seed: int = 0) -> dict:
    arg_keys = jax.random.split(jax.random.key(seed), 10)
    return {
        "features_t": bell_draw(arg_keys[0], (F_IN, NODES), 1.0, 6.0, ((0, 8), (1, 64))),
        "node_order": draw_node_order(jax.random.fold_in(arg_keys[9], 71), 0),
        "tile_rows": draw_tile_rows(jax.random.fold_in(arg_keys[9], 71), 0),
        "tile_cols": draw_tile_cols(jax.random.fold_in(arg_keys[9], 71), 0),
        "tile_vals": bell_draw(arg_keys[4], (N_COL, TILES, BLOCK, BLOCK), (BLOCK * TILES // (2 * COLBLK)) ** -0.5, 0.21875, ((0, 64),)),
        "tile_count": draw_tile_count(jax.random.fold_in(arg_keys[9], 71), 0),
        "weight": bell_draw(arg_keys[6], (F_IN, HID), F_IN ** -0.5, 0.5),
        "bias_term": bell_draw(arg_keys[7], (HID,), 0.5, 3.0, (), jnp.float32),
        "cotangent": bell_draw(arg_keys[8], (HID, NODES), 1.0, 6.0, ((1, 512),)),
    }


def reference(features_t, node_order, tile_rows, tile_cols, tile_vals, tile_count, weight, bias_term, cotangent):
    group_total = BLOCKS // COLBLK
    permuted = jnp.take(features_t, node_order, axis=1)
    perm_blocks = permuted.reshape(F_IN, BLOCKS, BLOCK)
    slot_index = jnp.arange(TILES, dtype=jnp.int32)
    group_ids = jnp.arange(group_total, dtype=jnp.int32)

    def forward_group(totals, inputs):
        row_ids, col_ids, blocks_in, live_count, group_id = inputs
        alive_mask = (slot_index < live_count).astype(jnp.float32)
        picked = jnp.take(perm_blocks, group_id * COLBLK + col_ids, axis=1).astype(jnp.float32)
        product = jnp.einsum('ftk,tjk->tfj', picked, blocks_in.astype(jnp.float32))
        product = product * alive_mask[:, None, None]
        return (totals.at[row_ids].add(product), None)
    start_sums = jnp.zeros((BLOCKS, F_IN, BLOCK), jnp.float32)
    sums, _ = lax.scan(forward_group, start_sums, (tile_rows, tile_cols, tile_vals, tile_count, group_ids))
    aggregated = sums.transpose(1, 0, 2).reshape(F_IN, NODES).astype(jnp.bfloat16)
    preact = jnp.dot(weight.T, aggregated, preferred_element_type=jnp.float32) + bias_term[:, None]
    act_value, pullback = jax.vjp(jax.nn.gelu, preact)
    activated = act_value.astype(jnp.bfloat16)
    grad_pre = pullback(cotangent.astype(jnp.float32))[0].astype(jnp.bfloat16)
    grad_weight = jnp.dot(aggregated, grad_pre.T, preferred_element_type=jnp.float32)
    grad_bias = lax.optimization_barrier(jnp.sum(grad_pre.astype(jnp.float32), axis=1))
    grad_agg = jnp.dot(weight, grad_pre, preferred_element_type=jnp.float32).astype(jnp.bfloat16)
    agg_blocks = grad_agg.reshape(F_IN, BLOCKS, BLOCK)

    def backward_group(carry, inputs):
        row_ids, col_ids, blocks_in, live_count = inputs
        alive_mask = (slot_index < live_count).astype(jnp.float32)
        picked = jnp.take(agg_blocks, row_ids, axis=1).astype(jnp.float32)
        product = jnp.einsum('ftj,tjk->tfk', picked, blocks_in.astype(jnp.float32))
        product = product * alive_mask[:, None, None]
        local_sums = jnp.zeros((COLBLK, F_IN, BLOCK), jnp.float32).at[col_ids].add(product)
        return (carry, local_sums)
    _, per_group = lax.scan(backward_group, jnp.zeros((), jnp.float32), (tile_rows, tile_cols, tile_vals, tile_count))
    grad_perm = per_group.transpose(2, 0, 1, 3).reshape(F_IN, NODES)
    grad_features = jnp.zeros((F_IN, NODES), jnp.float32).at[:, node_order].set(grad_perm).astype(jnp.bfloat16)
    return (activated, grad_weight, grad_bias, grad_features)
```

```python
import functools

import jax
import jax.numpy as jnp
from jax import lax
from jax.experimental import pallas as pl
from jax.experimental.pallas import tpu as pltpu
from jax.sharding import PartitionSpec as P

BF = jnp.bfloat16
F32 = jnp.float32
MESH = pl.DeviceIdType.MESH
NT = (((1,), (1,)), ((), ()))

BLOCK = 128
ROWS = 16
SLOTS = 96
RUN = 12
SIDE = 8
PAIRS = 128
HID = 256
F_IN = 128
NODES = 1024


def pair_of(row, group):
    return (row >> 3) * 2 + jnp.minimum((row - group) & 7, 1)


def one_hot(order_row):
    node = lax.broadcasted_iota(jnp.int32, (NODES, order_row.shape[1]), 0)
    return jnp.where(node == order_row, 1.0, 0.0).astype(BF)


def forward_kernel(
    rows_ref, cols_ref, count_ref, order_ref, feats_ref, vals_hbm, out_ref, vals, perm, acc, sems
):
    def copy(run):
        at = pl.ds(run * RUN, RUN)
        return pltpu.make_async_copy(vals_hbm.at[at], vals.at[at], sems.at[run])

    for run in range(SLOTS // RUN):
        copy(run).start()
    acc[...] = jnp.zeros_like(acc)
    group = lax.axis_index("col")
    order = order_ref[...] - group * NODES
    feats = feats_ref[...]
    for block in range(SIDE):
        at = slice(block * BLOCK, (block + 1) * BLOCK)
        perm[block] = jnp.dot(feats, one_hot(order[:, at]), preferred_element_type=F32).astype(BF)
    count = count_ref[0]

    def one_run(run, _):
        copy(run).wait()
        first = run * RUN
        products = []
        for step in range(RUN):
            slot = first + step
            product = lax.dot_general(
                perm[cols_ref[0, slot]], vals[slot], NT, preferred_element_type=F32
            )
            products.append(jnp.where(slot < count, product, 0.0))
        for step in range(RUN):
            place = pair_of(rows_ref[0, first + step], group)
            acc[place] += products[step]
        return 0

    lax.fori_loop(0, SLOTS // RUN, one_run, 0)
    out_ref[...] = acc[...].astype(BF)


def exchange_kernel(
    rows_ref,
    cols_ref,
    count_ref,
    order_ref,
    vals_hbm,
    part,
    weight_ref,
    bias_ref,
    cot_ref,
    act_ref,
    gw_ref,
    gb_ref,
    gf_ref,
    vals,
    from_y,
    sum_y,
    pieces,
    agg,
    grad_out,
    gath,
    terms,
    red_h,
    red_f,
    red_y,
    whole,
    vals_sem,
    a_send,
    a_recv,
    b_send,
    b_recv,
    c_send,
    c_recv,
    d_send,
    d_recv,
    r_send,
    r_recv,
):
    col = lax.axis_index("col")
    feat = lax.axis_index("feat")
    y = col // SIDE
    h = col % SIDE

    def y_peer(step):
        return (y + step) % SIDE

    def h_peer(step):
        return (h + step) % SIDE

    def f_peer(step):
        return (feat + step) % SIDE

    def is_self(q):
        return feat == (h + q) % SIDE

    barrier = pltpu.get_barrier_semaphore()

    def greet(at_col, at_feat):
        pl.semaphore_signal(barrier, inc=1, device_id=(at_col, at_feat), device_id_type=MESH)

    def greet_peers(step, _):
        greet(y_peer(step) * SIDE + h, feat)
        greet(y * SIDE + h_peer(step), feat)
        greet(col, f_peer(step))
        return 0

    lax.fori_loop(1, SIDE, greet_peers, 0)

    def greet_pairs(i, _):
        other, q = i // 2, i % 2

        @pl.when(jnp.logical_not(jnp.logical_and(is_self(q), other == h)))
        def _():
            greet(y * SIDE + other, (h + q) % SIDE)

        @pl.when(jnp.logical_not(jnp.logical_and(is_self(q), other == feat)))
        def _():
            greet(y * SIDE + (feat + SIDE - q) % SIDE, other)

        return 0

    lax.fori_loop(0, 2 * SIDE, greet_pairs, 0)

    vals_copy = pltpu.make_async_copy(vals_hbm, vals, vals_sem)
    vals_copy.start()
    weight = weight_ref[...]
    weight_t = weight.T
    bias = jnp.broadcast_to(bias_ref[...], (8, HID)).T[:, :1]

    selves = jnp.where(is_self(0), 1, 0) + jnp.where(is_self(1), 1, 0)
    pl.semaphore_wait(barrier, 3 * (SIDE - 1) + 4 * SIDE - 2 * selves)

    def a_copy(step):
        to = y_peer(step)
        return pltpu.make_async_remote_copy(
            src_ref=part.at[pl.ds(to * 2 * SIDE, 2 * SIDE)],
            dst_ref=from_y.at[step],
            send_sem=a_send.at[step],
            recv_sem=a_recv.at[step],
            device_id=(to * SIDE + h, feat),
            device_id_type=MESH,
        )

    for step in (4, 3, 5, 2, 6, 1, 7):
        a_copy(step).start()
    for step in (1, 7, 2, 6, 3, 5, 4):
        a_copy(step).wait_recv()

    def add_y(i, _):
        total = part[y * 2 * SIDE + i].astype(F32)
        for step in range(1, SIDE):
            total = total + from_y[step, i].astype(F32)
        sum_y[i] = total.astype(BF)
        return 0

    lax.fori_loop(0, 2 * SIDE, add_y, 0)

    def b_copy(i):
        other, q = i // 2, i % 2
        return pltpu.make_async_remote_copy(
            src_ref=sum_y.at[i],
            dst_ref=pieces.at[q * SIDE + feat],
            send_sem=b_send.at[i],
            recv_sem=b_recv.at[q * SIDE + feat],
            device_id=(y * SIDE + other, (h + q) % SIDE),
            device_id_type=MESH,
        )

    def b_here(i):
        return jnp.logical_and(is_self(i % 2), i // 2 == h)

    def b_start(i, _):
        @pl.when(b_here(i))
        def _():
            pieces[(i % 2) * SIDE + feat] = sum_y[i]

        @pl.when(jnp.logical_not(b_here(i)))
        def _():
            b_copy(i).start()

        return 0

    lax.fori_loop(0, 2 * SIDE, b_start, 0)

    def b_wait(i, _):
        q, source = i // SIDE, i % SIDE

        @pl.when(jnp.logical_not(jnp.logical_and(is_self(q), source == feat)))
        def _():
            pltpu.make_async_remote_copy(
                src_ref=sum_y.at[0],
                dst_ref=pieces.at[i],
                send_sem=b_send.at[0],
                recv_sem=b_recv.at[i],
                device_id=(y * SIDE + (feat + SIDE - q) % SIDE, source),
                device_id_type=MESH,
            ).wait_recv()

        return 0

    lax.fori_loop(0, 2 * SIDE, b_wait, 0)
    for i in range(SIDE):
        both = pieces[i].astype(F32) + pieces[SIDE + i].astype(F32)
        agg[i * ROWS : (i + 1) * ROWS, :] = both.astype(BF)

    aggregated = agg[...]
    pre = jnp.dot(weight_t, aggregated, preferred_element_type=F32) + bias
    root = 0.7978845608028654
    square = pre * pre
    bend = jnp.tanh(root * (pre + 0.044715 * (square * pre)))
    half = 0.5 * (1.0 + bend)
    act_ref[...] = (pre * half).astype(BF)
    slope = half + 0.5 * pre * (1.0 - bend * bend) * (root * (1.0 + 3.0 * 0.044715 * square))
    grad_pre = (cot_ref[...].astype(F32) * slope).astype(BF)
    grad_agg = jnp.dot(weight, grad_pre, preferred_element_type=F32).astype(BF)
    for i in range(SIDE):
        grad_out[i] = grad_agg[i * ROWS : (i + 1) * ROWS, :]

    def c_copy(i):
        other, q = i // 2, i % 2
        place = y * 2 * SIDE + h * 2 + q
        return pltpu.make_async_remote_copy(
            src_ref=grad_out.at[other],
            dst_ref=gath.at[place],
            send_sem=c_send.at[i],
            recv_sem=c_recv.at[h * 2 + q],
            device_id=(y * SIDE + (feat + SIDE - q) % SIDE, other),
            device_id_type=MESH,
        )

    def c_here(i):
        return jnp.logical_and(is_self(i % 2), i // 2 == feat)

    def c_start(i, _):
        @pl.when(c_here(i))
        def _():
            gath[y * 2 * SIDE + h * 2 + i % 2] = grad_out[feat]

        @pl.when(jnp.logical_not(c_here(i)))
        def _():
            c_copy(i).start()

        return 0

    lax.fori_loop(0, 2 * SIDE, c_start, 0)

    grad_w = lax.dot_general(aggregated, grad_pre, NT, preferred_element_type=F32)
    grad_b = lax.dot_general(jnp.ones((ROWS, BLOCK), BF), grad_pre, NT, preferred_element_type=F32)
    for i in range(SIDE):
        terms[i, :ROWS, :] = grad_w[i * ROWS : (i + 1) * ROWS, :]
        terms[i, ROWS:, :] = grad_b[:8, :]

    def r_copy(stage, step, src, dst, device):
        return pltpu.make_async_remote_copy(
            src_ref=src,
            dst_ref=dst,
            send_sem=r_send.at[stage, step],
            recv_sem=r_recv.at[stage, step],
            device_id=device,
            device_id_type=MESH,
        )

    def r_h(step):
        to = h_peer(step)
        return r_copy(0, step, terms.at[to], red_h.at[h], (y * SIDE + to, feat))

    def r_f(step):
        return r_copy(1, step, red_f.at[feat], red_f.at[feat], (col, f_peer(step)))

    def r_y(step):
        return r_copy(2, step, red_y.at[y], red_y.at[y], (y_peer(step) * SIDE + h, feat))

    def r_all(step):
        return r_copy(3, step, whole.at[h], whole.at[h], (y * SIDE + h_peer(step), feat))

    def r_start(make):
        def one(step, _):
            make(step).start()
            return 0

        lax.fori_loop(1, SIDE, one, 0)

    def r_wait(stage, buffer, place, device):
        def one(step, _):
            r_copy(stage, step, buffer.at[0], buffer.at[place(SIDE - step)], device).wait_recv()
            return 0

        lax.fori_loop(1, SIDE, one, 0)

    r_start(r_h)

    def c_wait(i, _):
        other, q = i // 2, i % 2

        @pl.when(jnp.logical_not(jnp.logical_and(is_self(q), other == h)))
        def _():
            pltpu.make_async_remote_copy(
                src_ref=grad_out.at[0],
                dst_ref=gath.at[y * 2 * SIDE + i],
                send_sem=c_send.at[0],
                recv_sem=c_recv.at[i],
                device_id=(y * SIDE + other, (h + q) % SIDE),
                device_id_type=MESH,
            ).wait_recv()

        return 0

    lax.fori_loop(0, 2 * SIDE, c_wait, 0)

    def d_copy(step):
        own = gath.at[pl.ds(y * 2 * SIDE, 2 * SIDE)]
        return pltpu.make_async_remote_copy(
            src_ref=own,
            dst_ref=own,
            send_sem=d_send.at[step],
            recv_sem=d_recv.at[step],
            device_id=(y_peer(step) * SIDE + h, feat),
            device_id_type=MESH,
        )

    for step in (4, 3, 5, 2, 6, 1, 7):
        d_copy(step).start()

    def total_of(buffer):
        total = buffer[0]
        for i in range(1, SIDE):
            total = total + buffer[i]
        return total

    red_h[h] = terms[h]
    r_wait(0, red_h, h_peer, (y * SIDE + h_peer(1), feat))
    red_f[feat] = total_of(red_h)
    r_start(r_f)
    r_wait(1, red_f, f_peer, (col, f_peer(1)))
    red_y[y] = total_of(red_f)
    r_start(r_y)
    r_wait(2, red_y, y_peer, (y_peer(1) * SIDE + h, feat))
    final = total_of(red_y)
    whole[h] = final[:ROWS, :]
    gb_ref[...] = final[ROWS : ROWS + 1, :]
    r_start(r_all)

    vals_copy.wait()
    for step in range(1, SIDE):
        pltpu.make_async_remote_copy(
            src_ref=gath.at[pl.ds(0, 2 * SIDE)],
            dst_ref=gath.at[pl.ds(y_peer(SIDE - step) * 2 * SIDE, 2 * SIDE)],
            send_sem=d_send.at[step],
            recv_sem=d_recv.at[step],
            device_id=(y_peer(1) * SIDE + h, feat),
            device_id_type=MESH,
        ).wait_recv()
    count = count_ref[0]

    def one_run(run, total):
        first = run * RUN
        wide = []
        for step in range(RUN):
            slot = first + step
            piece = gath[pair_of(rows_ref[0, slot], col)]
            where = jnp.where(slot < count, cols_ref[0, slot], -1)
            wide.append(
                jnp.concatenate(
                    [jnp.where(where == b, piece, jnp.zeros_like(piece)) for b in range(SIDE)], axis=0
                )
            )
        left = jnp.concatenate(wide, axis=1)
        right = vals[pl.ds(first, RUN)].reshape(RUN * BLOCK, BLOCK)
        return total + jnp.dot(left, right, preferred_element_type=F32)

    sums = lax.fori_loop(0, SLOTS // RUN, one_run, jnp.zeros((SIDE * ROWS, BLOCK), F32)).astype(BF)
    order = order_ref[...] - col * NODES
    out = jnp.zeros((ROWS, NODES), F32)
    for block in range(SIDE):
        out = out + lax.dot_general(
            sums[block * ROWS : (block + 1) * ROWS, :],
            one_hot(order[:, block * BLOCK : (block + 1) * BLOCK]),
            NT,
            preferred_element_type=F32,
        )
    gf_ref[...] = out.astype(BF)

    r_wait(3, whole, h_peer, (y * SIDE + h_peer(1), feat))
    gw_ref[...] = whole[...]

    for step in range(1, SIDE):
        a_copy(step).wait_send()
        d_copy(step).wait_send()

    def r_done(step, _):
        r_h(step).wait_send()
        r_f(step).wait_send()
        r_y(step).wait_send()
        r_all(step).wait_send()
        return 0

    lax.fori_loop(1, SIDE, r_done, 0)

    def pairs_done(i, _):
        @pl.when(jnp.logical_not(b_here(i)))
        def _():
            b_copy(i).wait_send()

        @pl.when(jnp.logical_not(c_here(i)))
        def _():
            c_copy(i).wait_send()

        return 0

    lax.fori_loop(0, 2 * SIDE, pairs_done, 0)


def per_device(
    features_t,
    node_order,
    tile_rows,
    tile_cols,
    tile_vals,
    tile_count,
    weight,
    bias_term,
    cotangent,
):
    vmem = pl.BlockSpec(memory_space=pltpu.VMEM)
    smem = pl.BlockSpec(memory_space=pltpu.SMEM)
    hbm = pl.BlockSpec(memory_space=pl.ANY)
    order = node_order.reshape(1, NODES)
    vals = tile_vals.reshape(SLOTS, BLOCK, BLOCK)
    part = pl.pallas_call(
        forward_kernel,
        out_shape=jax.ShapeDtypeStruct((PAIRS, ROWS, BLOCK), BF),
        in_specs=[smem, smem, smem, vmem, vmem, hbm],
        out_specs=vmem,
        scratch_shapes=[
            pltpu.VMEM((SLOTS, BLOCK, BLOCK), BF),
            pltpu.VMEM((SIDE, ROWS, BLOCK), BF),
            pltpu.VMEM((PAIRS, ROWS, BLOCK), F32),
            pltpu.SemaphoreType.DMA((SLOTS // RUN,)),
        ],
        compiler_params=pltpu.CompilerParams(vmem_limit_bytes=40 << 20),
        name="forward_tiles",
    )(tile_rows, tile_cols, tile_count, order, features_t, vals)

    dma = pltpu.SemaphoreType.DMA
    act, grad_w, grad_b, grad_f = pl.pallas_call(
        exchange_kernel,
        out_shape=(
            jax.ShapeDtypeStruct((HID, BLOCK), BF),
            jax.ShapeDtypeStruct((SIDE, ROWS, HID), F32),
            jax.ShapeDtypeStruct((1, HID), F32),
            jax.ShapeDtypeStruct((ROWS, NODES), BF),
        ),
        in_specs=[smem, smem, smem, vmem, hbm, vmem, vmem, vmem, vmem],
        out_specs=(vmem, vmem, vmem, vmem),
        scratch_shapes=[
            pltpu.VMEM((SLOTS, BLOCK, BLOCK), BF),
            pltpu.VMEM((SIDE, 2 * SIDE, ROWS, BLOCK), BF),
            pltpu.VMEM((2 * SIDE, ROWS, BLOCK), BF),
            pltpu.VMEM((2 * SIDE, ROWS, BLOCK), BF),
            pltpu.VMEM((F_IN, BLOCK), BF),
            pltpu.VMEM((SIDE, ROWS, BLOCK), BF),
            pltpu.VMEM((PAIRS, ROWS, BLOCK), BF),
            pltpu.VMEM((SIDE, ROWS + 8, HID), F32),
            pltpu.VMEM((SIDE, ROWS + 8, HID), F32),
            pltpu.VMEM((SIDE, ROWS + 8, HID), F32),
            pltpu.VMEM((SIDE, ROWS + 8, HID), F32),
            pltpu.VMEM((SIDE, ROWS, HID), F32),
            dma,
            dma((SIDE,)),
            dma((SIDE,)),
            dma((2 * SIDE,)),
            dma((2 * SIDE,)),
            dma((2 * SIDE,)),
            dma((2 * SIDE,)),
            dma((SIDE,)),
            dma((SIDE,)),
            dma((4, SIDE)),
            dma((4, SIDE)),
        ],
        compiler_params=pltpu.CompilerParams(
            collective_id=0, has_side_effects=True, vmem_limit_bytes=40 << 20
        ),
        name="exchange_layer",
    )(tile_rows, tile_cols, tile_count, order, vals, part, weight, bias_term.reshape(1, HID), cotangent)
    return act, grad_w.reshape(F_IN, HID), grad_b.reshape(HID), grad_f


def solution(mesh):
    return jax.shard_map(
        per_device,
        mesh=mesh,
        in_specs=(
            P("feat", "col"),
            P("col"),
            P("col", None),
            P("col", None),
            P("col", None, None, None),
            P("col"),
            P(),
            P(),
            P(None, ("col", "feat")),
        ),
        out_specs=(P(None, ("col", "feat")), P(), P(), P("feat", "col")),
        check_vma=False,
    )
```

```python
import jax
import jax.numpy as jnp
from jax import lax
from jax.experimental import pallas as pl
from jax.experimental.pallas import tpu as pltpu
from jax.sharding import PartitionSpec as P

BF = jnp.bfloat16
F32 = jnp.float32
MESH = pl.DeviceIdType.MESH
NT = (((1,), (1,)), ((), ()))

BLOCK = 128
ROWS = 16
SLOTS = 96
RUN = 12
SIDE = 8
PAIRS = 128
HID = 256
F_IN = 128
NODES = 1024
VMEM_BYTES = 60 << 20
STEPS = (4, 3, 5, 2, 6, 1, 7)
FAR_FIRST = (2, 1, 3, 0)
NEAR_FIRST = (0, 1, 3, 2)


def pair_of(row, group):
    return (row >> 3) * 2 + jnp.minimum((row - group) & 7, 1)


def one_hot(order_row):
    node = lax.broadcasted_iota(jnp.int32, (NODES, order_row.shape[1]), 0)
    return jnp.where(node == order_row, 1.0, 0.0).astype(BF)


def exchange_kernel(
    rows_hbm,
    cols_hbm,
    count_hbm,
    order_hbm,
    feats_hbm,
    vals_hbm,
    weight_hbm,
    bias_hbm,
    cot_hbm,
    act_hbm,
    gw_hbm,
    gb_hbm,
    gf_hbm,
    rows_ref,
    cols_ref,
    count_ref,
    rows_wide,
    order_ref,
    feats_ref,
    vals,
    weight_ref,
    bias_ref,
    cot_ref,
    hot,
    perm,
    products,
    totals,
    part,
    from_y,
    sum_y,
    pieces,
    agg,
    grad_out,
    gath,
    terms,
    red_y,
    red_f,
    red_h,
    whole,
    act_ref,
    gb_ref,
    gf_ref,
    out_sem,
    in_sem,
    vals_sem,
    a_send,
    a_recv,
    b_send,
    b_recv,
    c_send,
    c_recv,
    d_send,
    d_recv,
    r_send,
    r_recv,
):
    col = lax.axis_index("col")
    feat = lax.axis_index("feat")
    y = col // SIDE
    h = col % SIDE
    z = h // 2

    def vals_copy(run):
        at = pl.ds(run * RUN, RUN)
        return pltpu.make_async_copy(vals_hbm.at[at], vals.at[at], vals_sem.at[run])

    outputs = [
        pltpu.make_async_copy(src, dst, out_sem.at[i])
        for i, (src, dst) in enumerate(
            ((act_ref, act_hbm), (whole, gw_hbm), (gb_ref, gb_hbm), (gf_ref, gf_hbm))
        )
    ]
    inputs = [
        pltpu.make_async_copy(src, dst, in_sem.at[i])
        for i, (src, dst) in enumerate(
            (
                (order_hbm, order_ref),
                (feats_hbm, feats_ref),
                (rows_hbm, rows_ref),
                (cols_hbm, cols_ref),
                (rows_hbm, rows_wide),
                (count_hbm, count_ref),
                (weight_hbm, weight_ref),
                (bias_hbm, bias_ref),
                (cot_hbm, cot_ref),
            )
        )
    ]
    for copy in inputs[:6]:
        copy.start()
    for run in range(SLOTS // RUN):
        vals_copy(run).start()
    for copy in inputs[6:]:
        copy.start()

    def y_peer(step):
        return (y + step) % SIDE

    def h_peer(step):
        return (h + step) % SIDE

    def f_peer(step):
        return (feat + step) % SIDE

    def is_self(q):
        return feat == (h + q) % SIDE

    barrier = pltpu.get_barrier_semaphore()

    def greet(at_col, at_feat):
        pl.semaphore_signal(barrier, inc=1, device_id=(at_col, at_feat), device_id_type=MESH)

    def greet_peers(step, _):
        greet(y_peer(step) * SIDE + h, feat)
        greet(y * SIDE + h_peer(step), feat)
        greet(col, f_peer(step))
        return 0

    lax.fori_loop(1, SIDE, greet_peers, 0)

    def greet_pairs(i, _):
        other, q = i // 2, i % 2

        @pl.when(jnp.logical_not(jnp.logical_and(is_self(q), other == h)))
        def _():
            greet(y * SIDE + other, (h + q) % SIDE)

        @pl.when(jnp.logical_not(jnp.logical_and(is_self(q), other == feat)))
        def _():
            greet(y * SIDE + (feat + SIDE - q) % SIDE, other)

        return 0

    lax.fori_loop(0, 2 * SIDE, greet_pairs, 0)

    inputs[0].wait()
    inputs[1].wait()
    order = order_ref[...] - col * NODES
    feats = feats_ref[...]
    for block in range(SIDE):
        at = slice(block * BLOCK, (block + 1) * BLOCK)
        hot[:, at] = one_hot(order[:, at])
        perm[block] = jnp.dot(feats, hot[:, at], preferred_element_type=F32).astype(BF)

    for copy in inputs[2:6]:
        copy.wait()
    count = count_ref[0]

    def one_forward(run, _):
        vals_copy(run).wait()
        for step in range(RUN):
            slot = run * RUN + step
            products[pl.ds(pl.multiple_of(slot * ROWS, ROWS), ROWS), :] = lax.dot_general(
                perm[cols_ref[0, slot]], vals[slot], NT, preferred_element_type=F32
            )
        return 0

    lax.fori_loop(0, SLOTS // RUN, one_forward, 0)
    place = pair_of(rows_wide[...], col)
    place = jnp.where(lax.broadcasted_iota(jnp.int32, (1, SLOTS), 1) < count, place, -1)
    pick = jnp.where(lax.broadcasted_iota(jnp.int32, (PAIRS, SLOTS), 0) == place, 1.0, 0.0).astype(BF)
    for f in range(ROWS):
        value = products[pl.ds(f, SLOTS, stride=ROWS), :]
        high = value.astype(BF)
        low = (value - high.astype(F32)).astype(BF)
        totals[pl.ds(f, PAIRS, stride=ROWS), :] = jnp.dot(
            pick, high, preferred_element_type=F32
        ) + jnp.dot(pick, low, preferred_element_type=F32)
    part[...] = totals[...].reshape(PAIRS, ROWS, BLOCK).astype(BF)

    for copy in inputs[6:]:
        copy.wait()
    weight = weight_ref[...]
    weight_t = weight.T
    bias = jnp.broadcast_to(bias_ref[...], (8, HID)).T[:, :1]

    selves = jnp.where(is_self(0), 1, 0) + jnp.where(is_self(1), 1, 0)
    pl.semaphore_wait(barrier, 3 * (SIDE - 1) + 4 * SIDE - 2 * selves)

    def a_copy(turn, step):
        to = y_peer(step)
        at = (z + turn) % 4 * 4
        return pltpu.make_async_remote_copy(
            src_ref=part.at[pl.ds(to * 2 * SIDE + at, 4)],
            dst_ref=from_y.at[step, pl.ds(at, 4)],
            send_sem=a_send.at[turn, step],
            recv_sem=a_recv.at[turn, step],
            device_id=(to * SIDE + h, feat),
            device_id_type=MESH,
        )

    for turn in FAR_FIRST:
        for step in STEPS:
            a_copy(turn, step).start()

    def b_copy(i):
        other, q = i // 2, i % 2
        return pltpu.make_async_remote_copy(
            src_ref=sum_y.at[i],
            dst_ref=pieces.at[q * SIDE + feat],
            send_sem=b_send.at[i],
            recv_sem=b_recv.at[q * SIDE + feat],
            device_id=(y * SIDE + other, (h + q) % SIDE),
            device_id_type=MESH,
        )

    def b_here(i):
        return jnp.logical_and(is_self(i % 2), i // 2 == h)

    for turn in FAR_FIRST:
        for step in range(1, SIDE):
            a_copy(turn, step).wait_recv()

        def b_start(k, _, turn=turn):
            i = (z + turn) % 4 * 4 + k
            total = part[y * 2 * SIDE + i].astype(F32)
            for step in range(1, SIDE):
                total = total + from_y[step, i].astype(F32)
            sum_y[i] = total.astype(BF)

            @pl.when(b_here(i))
            def _():
                pieces[(i % 2) * SIDE + feat] = sum_y[i]

            @pl.when(jnp.logical_not(b_here(i)))
            def _():
                b_copy(i).start()

            return 0

        lax.fori_loop(0, 4, b_start, 0)

    def b_wait(i, _):
        q, source = i // SIDE, i % SIDE

        @pl.when(jnp.logical_not(jnp.logical_and(is_self(q), source == feat)))
        def _():
            pltpu.make_async_remote_copy(
                src_ref=sum_y.at[0],
                dst_ref=pieces.at[i],
                send_sem=b_send.at[0],
                recv_sem=b_recv.at[i],
                device_id=(y * SIDE + (feat + SIDE - q) % SIDE, source),
                device_id_type=MESH,
            ).wait_recv()

        return 0

    lax.fori_loop(0, 2 * SIDE, b_wait, 0)
    for i in range(SIDE):
        both = pieces[i].astype(F32) + pieces[SIDE + i].astype(F32)
        agg[i * ROWS : (i + 1) * ROWS, :] = both.astype(BF)

    aggregated = agg[...]
    pre = jnp.dot(weight_t, aggregated, preferred_element_type=F32) + bias
    root = 0.7978845608028654
    square = pre * pre
    bend = jnp.tanh(root * (pre + 0.044715 * (square * pre)))
    half = 0.5 * (1.0 + bend)
    act_ref[...] = (pre * half).astype(BF)
    slope = half + 0.5 * pre * (1.0 - bend * bend) * (root * (1.0 + 3.0 * 0.044715 * square))
    grad_pre = (cot_ref[...].astype(F32) * slope).astype(BF)
    grad_agg = jnp.dot(weight, grad_pre, preferred_element_type=F32).astype(BF)
    for i in range(SIDE):
        grad_out[i] = grad_agg[i * ROWS : (i + 1) * ROWS, :]

    def c_copy(i):
        other, q = i // 2, i % 2
        place = y * 2 * SIDE + h * 2 + q
        return pltpu.make_async_remote_copy(
            src_ref=grad_out.at[other],
            dst_ref=gath.at[place],
            send_sem=c_send.at[i],
            recv_sem=c_recv.at[h * 2 + q],
            device_id=(y * SIDE + (feat + SIDE - q) % SIDE, other),
            device_id_type=MESH,
        )

    def c_here(i):
        return jnp.logical_and(is_self(i % 2), i // 2 == feat)

    def c_start(i, _):
        @pl.when(c_here(i))
        def _():
            gath[y * 2 * SIDE + h * 2 + i % 2] = grad_out[feat]

        @pl.when(jnp.logical_not(c_here(i)))
        def _():
            c_copy(i).start()

        return 0

    lax.fori_loop(0, 2 * SIDE, c_start, 0)

    grad_w = lax.dot_general(aggregated, grad_pre, NT, preferred_element_type=F32)
    grad_b = lax.dot_general(jnp.ones((ROWS, BLOCK), BF), grad_pre, NT, preferred_element_type=F32)
    for i in range(SIDE):
        terms[i, :ROWS, :] = grad_w[i * ROWS : (i + 1) * ROWS, :]
        terms[i, ROWS:, :] = grad_b[:8, :]

    def r_copy(stage, step, src, dst, device):
        return pltpu.make_async_remote_copy(
            src_ref=src,
            dst_ref=dst,
            send_sem=r_send.at[stage, step],
            recv_sem=r_recv.at[stage, step],
            device_id=device,
            device_id_type=MESH,
        )

    def r_y(step):
        to = y_peer(step)
        return r_copy(0, step, terms.at[to], red_y.at[y], (to * SIDE + h, feat))

    def r_f(step):
        return r_copy(1, step, red_f.at[feat], red_f.at[feat], (col, f_peer(step)))

    def r_h(step):
        return r_copy(2, step, red_h.at[h], red_h.at[h], (y * SIDE + h_peer(step), feat))

    def r_all(step):
        return r_copy(3, step, whole.at[y], whole.at[y], (y_peer(step) * SIDE + h, feat))

    def r_start(make):
        def one(step, _):
            make(step).start()
            return 0

        lax.fori_loop(1, SIDE, one, 0)

    def r_wait(stage, buffer, place, device):
        def one(step, _):
            r_copy(stage, step, buffer.at[0], buffer.at[place(SIDE - step)], device).wait_recv()
            return 0

        lax.fori_loop(1, SIDE, one, 0)

    r_start(r_y)
    outputs[0].start()

    def c_wait(i, _):
        other, q = i // 2, i % 2

        @pl.when(jnp.logical_not(jnp.logical_and(is_self(q), other == h)))
        def _():
            pltpu.make_async_remote_copy(
                src_ref=grad_out.at[0],
                dst_ref=gath.at[y * 2 * SIDE + i],
                send_sem=c_send.at[0],
                recv_sem=c_recv.at[i],
                device_id=(y * SIDE + other, (h + q) % SIDE),
                device_id_type=MESH,
            ).wait_recv()

        return 0

    def d_copy(turn, step):
        own = gath.at[pl.ds(y * 2 * SIDE + (z + turn) % 4 * 4, 4)]
        return pltpu.make_async_remote_copy(
            src_ref=own,
            dst_ref=own,
            send_sem=d_send.at[turn, step],
            recv_sem=d_recv.at[turn, step],
            device_id=(y_peer(step) * SIDE + h, feat),
            device_id_type=MESH,
        )

    for turn in NEAR_FIRST:
        first = (z + turn) % 4 * 4
        lax.fori_loop(first, first + 4, c_wait, 0)
        for step in STEPS:
            d_copy(turn, step).start()

    def total_of(buffer):
        total = buffer[0]
        for i in range(1, SIDE):
            total = total + buffer[i]
        return total

    red_y[y] = terms[y]
    r_wait(0, red_y, y_peer, (y_peer(1) * SIDE + h, feat))
    red_f[feat] = total_of(red_y)
    r_start(r_f)
    r_wait(1, red_f, f_peer, (col, f_peer(1)))
    red_h[h] = total_of(red_f)
    r_start(r_h)
    r_wait(2, red_h, h_peer, (y * SIDE + h_peer(1), feat))
    final = total_of(red_h)
    whole[y] = final[:ROWS, :]
    gb_ref[...] = final[ROWS : ROWS + 1, :]
    r_start(r_all)
    outputs[2].start()

    for turn in NEAR_FIRST:
        for step in range(1, SIDE):
            pltpu.make_async_remote_copy(
                src_ref=gath.at[pl.ds(0, 4)],
                dst_ref=gath.at[pl.ds(y_peer(SIDE - step) * 2 * SIDE + (z + turn) % 4 * 4, 4)],
                send_sem=d_send.at[turn, step],
                recv_sem=d_recv.at[turn, step],
                device_id=(y_peer(1) * SIDE + h, feat),
                device_id_type=MESH,
            ).wait_recv()

    def one_run(run, total):
        first = run * RUN
        wide = []
        for step in range(RUN):
            slot = first + step
            piece = gath[pair_of(rows_ref[0, slot], col)]
            where = jnp.where(slot < count, cols_ref[0, slot], -1)
            wide.append(
                jnp.concatenate(
                    [jnp.where(where == b, piece, jnp.zeros_like(piece)) for b in range(SIDE)], axis=0
                )
            )
        left = jnp.concatenate(wide, axis=1)
        right = vals[pl.ds(first, RUN)].reshape(RUN * BLOCK, BLOCK)
        return total + jnp.dot(left, right, preferred_element_type=F32)

    sums = lax.fori_loop(0, SLOTS // RUN, one_run, jnp.zeros((SIDE * ROWS, BLOCK), F32)).astype(BF)
    out = jnp.zeros((ROWS, NODES), F32)
    for block in range(SIDE):
        out = out + lax.dot_general(
            sums[block * ROWS : (block + 1) * ROWS, :],
            hot[:, block * BLOCK : (block + 1) * BLOCK],
            NT,
            preferred_element_type=F32,
        )
    gf_ref[...] = out.astype(BF)
    outputs[3].start()

    r_wait(3, whole, y_peer, (y_peer(1) * SIDE + h, feat))
    outputs[1].start()

    for copy in outputs:
        copy.wait()
    for turn in range(4):
        for step in range(1, SIDE):
            a_copy(turn, step).wait_send()
            d_copy(turn, step).wait_send()

    def r_done(step, _):
        r_h(step).wait_send()
        r_f(step).wait_send()
        r_y(step).wait_send()
        r_all(step).wait_send()
        return 0

    lax.fori_loop(1, SIDE, r_done, 0)

    def pairs_done(i, _):
        @pl.when(jnp.logical_not(b_here(i)))
        def _():
            b_copy(i).wait_send()

        @pl.when(jnp.logical_not(c_here(i)))
        def _():
            c_copy(i).wait_send()

        return 0

    lax.fori_loop(0, 2 * SIDE, pairs_done, 0)


def write_kernel(*refs):
    sources, targets, sems = refs[:4], refs[4:8], refs[8]
    copies = [
        pltpu.make_async_copy(source, target, sems.at[i])
        for i, (source, target) in enumerate(zip(sources, targets))
    ]
    for copy in copies:
        copy.start()
    for copy in copies:
        copy.wait()


def per_device(
    features_t,
    node_order,
    tile_rows,
    tile_cols,
    tile_vals,
    tile_count,
    weight,
    bias_term,
    cotangent,
):
    hbm = pl.BlockSpec(memory_space=pl.ANY)
    dma = pltpu.SemaphoreType.DMA
    outs = (
        jax.ShapeDtypeStruct((HID, BLOCK), BF),
        jax.ShapeDtypeStruct((SIDE, ROWS, HID), F32),
        jax.ShapeDtypeStruct((1, HID), F32),
        jax.ShapeDtypeStruct((ROWS, NODES), BF),
    )
    made = pl.pallas_call(
        exchange_kernel,
        out_shape=outs,
        in_specs=[hbm] * 9,
        out_specs=(hbm,) * 4,
        scratch_shapes=[
            pltpu.SMEM((1, SLOTS), jnp.int32),
            pltpu.SMEM((1, SLOTS), jnp.int32),
            pltpu.SMEM((1,), jnp.int32),
            pltpu.VMEM((1, SLOTS), jnp.int32),
            pltpu.VMEM((1, NODES), jnp.int32),
            pltpu.VMEM((ROWS, NODES), BF),
            pltpu.VMEM((SLOTS, BLOCK, BLOCK), BF),
            pltpu.VMEM((F_IN, HID), BF),
            pltpu.VMEM((1, HID), F32),
            pltpu.VMEM((HID, BLOCK), BF),
            pltpu.VMEM((NODES, NODES), BF),
            pltpu.VMEM((SIDE, ROWS, BLOCK), BF),
            pltpu.VMEM((SLOTS * ROWS, BLOCK), F32),
            pltpu.VMEM((PAIRS * ROWS, BLOCK), F32),
            pltpu.VMEM((PAIRS, ROWS, BLOCK), BF),
            pltpu.VMEM((SIDE, 2 * SIDE, ROWS, BLOCK), BF),
            pltpu.VMEM((2 * SIDE, ROWS, BLOCK), BF),
            pltpu.VMEM((2 * SIDE, ROWS, BLOCK), BF),
            pltpu.VMEM((F_IN, BLOCK), BF),
            pltpu.VMEM((SIDE, ROWS, BLOCK), BF),
            pltpu.VMEM((PAIRS, ROWS, BLOCK), BF),
            pltpu.VMEM((SIDE, ROWS + 8, HID), F32),
            pltpu.VMEM((SIDE, ROWS + 8, HID), F32),
            pltpu.VMEM((SIDE, ROWS + 8, HID), F32),
            pltpu.VMEM((SIDE, ROWS + 8, HID), F32),
            pltpu.VMEM((SIDE, ROWS, HID), F32),
            pltpu.VMEM((HID, BLOCK), BF),
            pltpu.VMEM((1, HID), F32),
            pltpu.VMEM((ROWS, NODES), BF),
            dma((4,)),
            dma((9,)),
            dma((SLOTS // RUN,)),
            dma((4, SIDE)),
            dma((4, SIDE)),
            dma((2 * SIDE,)),
            dma((2 * SIDE,)),
            dma((2 * SIDE,)),
            dma((2 * SIDE,)),
            dma((4, SIDE)),
            dma((4, SIDE)),
            dma((4, SIDE)),
            dma((4, SIDE)),
        ],
        compiler_params=pltpu.CompilerParams(
            collective_id=0, has_side_effects=True, vmem_limit_bytes=VMEM_BYTES
        ),
        name="exchange_layer",
    )(
        tile_rows,
        tile_cols,
        tile_count,
        node_order.reshape(1, NODES),
        features_t,
        tile_vals.reshape(SLOTS, BLOCK, BLOCK),
        weight,
        bias_term.reshape(1, HID),
        cotangent,
    )
    act, grad_w, grad_b, grad_f = pl.pallas_call(
        write_kernel,
        out_shape=outs,
        in_specs=[hbm] * 4,
        out_specs=(hbm,) * 4,
        scratch_shapes=[dma((4,))],
        compiler_params=pltpu.CompilerParams(vmem_limit_bytes=VMEM_BYTES),
        name="write_outputs",
    )(*made)
    return act, grad_w.reshape(F_IN, HID), grad_b.reshape(HID), grad_f


def solution(mesh):
    return jax.shard_map(
        per_device,
        mesh=mesh,
        in_specs=(
            P("feat", "col"),
            P("col"),
            P("col", None),
            P("col", None),
            P("col", None, None, None),
            P("col"),
            P(),
            P(),
            P(None, ("col", "feat")),
        ),
        out_specs=(P(None, ("col", "feat")), P(), P(), P("feat", "col")),
        check_vma=False,
    )
```

```python
import jax
import jax.numpy as jnp
from jax import lax
from jax.experimental import pallas as pl
from jax.experimental.pallas import tpu as pltpu
from jax.sharding import PartitionSpec as P

BF = jnp.bfloat16
F32 = jnp.float32
MESH = pl.DeviceIdType.MESH
NT = (((1,), (1,)), ((), ()))

BLOCK = 128
ROWS = 16
SLOTS = 96
RUN = 12
SIDE = 8
PAIRS = 128
HID = 256
F_IN = 128
NODES = 1024
VMEM_BYTES = 40 << 20
STEPS = (4, 3, 5, 2, 6, 1, 7)
FAR_FIRST = (2, 1, 3, 0)
WINDOW = 2
NEAR_FIRST = (0, 1, 3, 2)


def pair_of(row, group):
    return (row >> 3) * 2 + jnp.minimum((row - group) & 7, 1)


def one_hot(order_row):
    node = lax.broadcasted_iota(jnp.int32, (NODES, order_row.shape[1]), 0)
    return jnp.where(node == order_row, 1.0, 0.0).astype(BF)


def exchange_kernel(
    rows_hbm,
    cols_hbm,
    count_hbm,
    order_hbm,
    feats_hbm,
    vals_hbm,
    weight_hbm,
    bias_hbm,
    cot_hbm,
    act_ref,
    gw_ref,
    gb_ref,
    gf_ref,
    rows_ref,
    cols_ref,
    count_ref,
    rows_wide,
    order_ref,
    feats_ref,
    vals,
    weight_ref,
    bias_ref,
    cot_ref,
    hot,
    perm,
    products,
    totals,
    part,
    from_y,
    sum_y,
    pieces,
    agg,
    grad_out,
    gath,
    terms,
    red_y,
    red_f,
    red_h,
    whole,
    in_sem,
    vals_sem,
    a_send,
    a_recv,
    b_send,
    b_recv,
    c_send,
    c_recv,
    d_send,
    d_recv,
    r_send,
    r_recv,
):
    col = lax.axis_index("col")
    feat = lax.axis_index("feat")
    y = col // SIDE
    h = col % SIDE
    z = h // 2

    def vals_copy(run):
        at = pl.ds(run * RUN, RUN)
        return pltpu.make_async_copy(vals_hbm.at[at], vals.at[at], vals_sem.at[run])

    inputs = [
        pltpu.make_async_copy(src, dst, in_sem.at[i])
        for i, (src, dst) in enumerate(
            (
                (order_hbm, order_ref),
                (feats_hbm, feats_ref),
                (rows_hbm, rows_ref),
                (cols_hbm, cols_ref),
                (rows_hbm, rows_wide),
                (count_hbm, count_ref),
                (weight_hbm, weight_ref),
                (bias_hbm, bias_ref),
                (cot_hbm, cot_ref),
            )
        )
    ]
    for copy in inputs[:6]:
        copy.start()
    for run in range(SLOTS // RUN):
        vals_copy(run).start()
    for copy in inputs[6:]:
        copy.start()

    def y_peer(step):
        return (y + step) % SIDE

    def h_peer(step):
        return (h + step) % SIDE

    def f_peer(step):
        return (feat + step) % SIDE

    def is_self(q):
        return feat == (h + q) % SIDE

    barrier = pltpu.get_barrier_semaphore()

    def greet(at_col, at_feat):
        pl.semaphore_signal(barrier, inc=1, device_id=(at_col, at_feat), device_id_type=MESH)

    def greet_peers(step, _):
        greet(y_peer(step) * SIDE + h, feat)
        greet(y * SIDE + h_peer(step), feat)
        greet(col, f_peer(step))
        return 0

    lax.fori_loop(1, SIDE, greet_peers, 0)

    def greet_pairs(i, _):
        other, q = i // 2, i % 2

        @pl.when(jnp.logical_not(jnp.logical_and(is_self(q), other == h)))
        def _():
            greet(y * SIDE + other, (h + q) % SIDE)

        @pl.when(jnp.logical_not(jnp.logical_and(is_self(q), other == feat)))
        def _():
            greet(y * SIDE + (feat + SIDE - q) % SIDE, other)

        return 0

    lax.fori_loop(0, 2 * SIDE, greet_pairs, 0)

    inputs[0].wait()
    inputs[1].wait()
    order = order_ref[...] - col * NODES
    feats = feats_ref[...]
    for block in range(SIDE):
        at = slice(block * BLOCK, (block + 1) * BLOCK)
        hot[:, at] = one_hot(order[:, at])
        perm[block] = jnp.dot(feats, hot[:, at], preferred_element_type=F32).astype(BF)

    for copy in inputs[2:6]:
        copy.wait()
    count = count_ref[0]

    def one_forward(run, _):
        vals_copy(run).wait()
        for step in range(RUN):
            slot = run * RUN + step
            products[pl.ds(pl.multiple_of(slot * ROWS, ROWS), ROWS), :] = lax.dot_general(
                perm[cols_ref[0, slot]], vals[slot], NT, preferred_element_type=F32
            )
        return 0

    lax.fori_loop(0, SLOTS // RUN, one_forward, 0)
    place = pair_of(rows_wide[...], col)
    place = jnp.where(lax.broadcasted_iota(jnp.int32, (1, SLOTS), 1) < count, place, -1)
    pick = jnp.where(lax.broadcasted_iota(jnp.int32, (PAIRS, SLOTS), 0) == place, 1.0, 0.0).astype(BF)
    for f in range(ROWS):
        value = products[pl.ds(f, SLOTS, stride=ROWS), :]
        high = value.astype(BF)
        low = (value - high.astype(F32)).astype(BF)
        totals[pl.ds(f, PAIRS, stride=ROWS), :] = jnp.dot(
            pick, high, preferred_element_type=F32
        ) + jnp.dot(pick, low, preferred_element_type=F32)
    part[...] = totals[...].reshape(PAIRS, ROWS, BLOCK).astype(BF)

    for copy in inputs[6:]:
        copy.wait()
    weight = weight_ref[...]
    weight_t = weight.T
    bias = jnp.broadcast_to(bias_ref[...], (8, HID)).T[:, :1]

    selves = jnp.where(is_self(0), 1, 0) + jnp.where(is_self(1), 1, 0)
    pl.semaphore_wait(barrier, 3 * (SIDE - 1) + 4 * SIDE - 2 * selves)

    def a_copy(turn, step):
        to = y_peer(step)
        at = (z + turn) % 4 * 4
        return pltpu.make_async_remote_copy(
            src_ref=part.at[pl.ds(to * 2 * SIDE + at, 4)],
            dst_ref=from_y.at[step, pl.ds(at, 4)],
            send_sem=a_send.at[turn, step],
            recv_sem=a_recv.at[turn, step],
            device_id=(to * SIDE + h, feat),
            device_id_type=MESH,
        )

    for turn in FAR_FIRST[:WINDOW]:
        for step in STEPS:
            a_copy(turn, step).start()

    def b_copy(i):
        other, q = i // 2, i % 2
        return pltpu.make_async_remote_copy(
            src_ref=sum_y.at[i],
            dst_ref=pieces.at[q * SIDE + feat],
            send_sem=b_send.at[i],
            recv_sem=b_recv.at[q * SIDE + feat],
            device_id=(y * SIDE + other, (h + q) % SIDE),
            device_id_type=MESH,
        )

    def b_here(i):
        return jnp.logical_and(is_self(i % 2), i // 2 == h)

    for nth, turn in enumerate(FAR_FIRST):
        if nth + WINDOW < 4:
            for step in STEPS:
                a_copy(turn, step).wait_send()
                a_copy(FAR_FIRST[nth + WINDOW], step).start()
        for step in range(1, SIDE):
            a_copy(turn, step).wait_recv()

        def b_start(k, _, turn=turn):
            i = (z + turn) % 4 * 4 + k
            total = part[y * 2 * SIDE + i].astype(F32)
            for step in range(1, SIDE):
                total = total + from_y[step, i].astype(F32)
            sum_y[i] = total.astype(BF)

            @pl.when(b_here(i))
            def _():
                pieces[(i % 2) * SIDE + feat] = sum_y[i]

            @pl.when(jnp.logical_not(b_here(i)))
            def _():
                b_copy(i).start()

            return 0

        lax.fori_loop(0, 4, b_start, 0)

    def b_wait(i, _):
        q, source = i // SIDE, i % SIDE

        @pl.when(jnp.logical_not(jnp.logical_and(is_self(q), source == feat)))
        def _():
            pltpu.make_async_remote_copy(
                src_ref=sum_y.at[0],
                dst_ref=pieces.at[i],
                send_sem=b_send.at[0],
                recv_sem=b_recv.at[i],
                device_id=(y * SIDE + (feat + SIDE - q) % SIDE, source),
                device_id_type=MESH,
            ).wait_recv()

        return 0

    lax.fori_loop(0, 2 * SIDE, b_wait, 0)
    for i in range(SIDE):
        both = pieces[i].astype(F32) + pieces[SIDE + i].astype(F32)
        agg[i * ROWS : (i + 1) * ROWS, :] = both.astype(BF)

    aggregated = agg[...]
    pre = jnp.dot(weight_t, aggregated, preferred_element_type=F32) + bias
    root = 0.7978845608028654
    square = pre * pre
    bend = jnp.tanh(root * (pre + 0.044715 * (square * pre)))
    half = 0.5 * (1.0 + bend)
    act_ref[...] = (pre * half).astype(BF)
    slope = half + 0.5 * pre * (1.0 - bend * bend) * (root * (1.0 + 3.0 * 0.044715 * square))
    grad_pre = (cot_ref[...].astype(F32) * slope).astype(BF)
    grad_agg = jnp.dot(weight, grad_pre, preferred_element_type=F32).astype(BF)
    for i in range(SIDE):
        grad_out[i] = grad_agg[i * ROWS : (i + 1) * ROWS, :]

    def c_copy(i):
        other, q = i // 2, i % 2
        place = y * 2 * SIDE + h * 2 + q
        return pltpu.make_async_remote_copy(
            src_ref=grad_out.at[other],
            dst_ref=gath.at[place],
            send_sem=c_send.at[i],
            recv_sem=c_recv.at[h * 2 + q],
            device_id=(y * SIDE + (feat + SIDE - q) % SIDE, other),
            device_id_type=MESH,
        )

    def c_here(i):
        return jnp.logical_and(is_self(i % 2), i // 2 == feat)

    def c_start(i, _):
        @pl.when(c_here(i))
        def _():
            gath[y * 2 * SIDE + h * 2 + i % 2] = grad_out[feat]

        @pl.when(jnp.logical_not(c_here(i)))
        def _():
            c_copy(i).start()

        return 0

    lax.fori_loop(0, 2 * SIDE, c_start, 0)

    grad_w = lax.dot_general(aggregated, grad_pre, NT, preferred_element_type=F32)
    grad_b = lax.dot_general(jnp.ones((ROWS, BLOCK), BF), grad_pre, NT, preferred_element_type=F32)
    upper = lax.broadcasted_iota(jnp.int32, (8, BLOCK), 0) < 4
    grad_b_tile = jnp.where(upper, grad_b[:8, :BLOCK], grad_b[:8, BLOCK:])
    for i in range(SIDE):
        for half in range(2):
            at = slice(half * BLOCK, (half + 1) * BLOCK)
            terms[i, half * ROWS : (half + 1) * ROWS, :] = grad_w[i * ROWS : (i + 1) * ROWS, at]
        terms[i, 2 * ROWS :, :] = grad_b_tile

    def r_copy(stage, step, src, dst, device):
        return pltpu.make_async_remote_copy(
            src_ref=src,
            dst_ref=dst,
            send_sem=r_send.at[stage, step],
            recv_sem=r_recv.at[stage, step],
            device_id=device,
            device_id_type=MESH,
        )

    def r_y(step):
        to = y_peer(step)
        return r_copy(0, step, terms.at[to], red_y.at[y], (to * SIDE + h, feat))

    def r_f(step):
        return r_copy(1, step, red_f.at[feat], red_f.at[feat], (col, f_peer(step)))

    def r_h(step):
        return r_copy(2, step, red_h.at[h], red_h.at[h], (y * SIDE + h_peer(step), feat))

    def r_all(step):
        return r_copy(3, step, whole.at[y], whole.at[y], (y_peer(step) * SIDE + h, feat))

    def r_start(make):
        def one(step, _):
            make(step).start()
            return 0

        lax.fori_loop(1, SIDE, one, 0)

    def r_wait(stage, buffer, place, device):
        def one(step, _):
            r_copy(stage, step, buffer.at[0], buffer.at[place(SIDE - step)], device).wait_recv()
            return 0

        lax.fori_loop(1, SIDE, one, 0)

    r_start(r_y)

    def c_wait(i, _):
        other, q = i // 2, i % 2

        @pl.when(jnp.logical_not(jnp.logical_and(is_self(q), other == h)))
        def _():
            pltpu.make_async_remote_copy(
                src_ref=grad_out.at[0],
                dst_ref=gath.at[y * 2 * SIDE + i],
                send_sem=c_send.at[0],
                recv_sem=c_recv.at[i],
                device_id=(y * SIDE + other, (h + q) % SIDE),
                device_id_type=MESH,
            ).wait_recv()

        return 0

    def d_copy(turn, step):
        own = gath.at[pl.ds(y * 2 * SIDE + (z + turn) % 4 * 4, 4)]
        return pltpu.make_async_remote_copy(
            src_ref=own,
            dst_ref=own,
            send_sem=d_send.at[turn, step],
            recv_sem=d_recv.at[turn, step],
            device_id=(y_peer(step) * SIDE + h, feat),
            device_id_type=MESH,
        )

    for turn in NEAR_FIRST:
        first = (z + turn) % 4 * 4
        lax.fori_loop(first, first + 4, c_wait, 0)
        for step in STEPS:
            d_copy(turn, step).start()

    def total_of(buffer):
        total = buffer[0]
        for i in range(1, SIDE):
            total = total + buffer[i]
        return total

    red_y[y] = terms[y]
    r_wait(0, red_y, y_peer, (y_peer(1) * SIDE + h, feat))
    red_f[feat] = total_of(red_y)
    r_start(r_f)
    r_wait(1, red_f, f_peer, (col, f_peer(1)))
    red_h[h] = total_of(red_f)
    r_start(r_h)
    r_wait(2, red_h, h_peer, (y * SIDE + h_peer(1), feat))
    final = total_of(red_h)
    for half in range(2):
        at = slice(half * BLOCK, (half + 1) * BLOCK)
        whole[y, :, at] = final[half * ROWS : (half + 1) * ROWS, :]
        gb_ref[:, at] = final[2 * ROWS + 4 * half : 2 * ROWS + 4 * half + 1, :]
    r_start(r_all)

    for turn in NEAR_FIRST:
        for step in range(1, SIDE):
            pltpu.make_async_remote_copy(
                src_ref=gath.at[pl.ds(0, 4)],
                dst_ref=gath.at[pl.ds(y_peer(SIDE - step) * 2 * SIDE + (z + turn) % 4 * 4, 4)],
                send_sem=d_send.at[turn, step],
                recv_sem=d_recv.at[turn, step],
                device_id=(y_peer(1) * SIDE + h, feat),
                device_id_type=MESH,
            ).wait_recv()

    def one_run(run, total):
        first = run * RUN
        wide = []
        for step in range(RUN):
            slot = first + step
            piece = gath[pair_of(rows_ref[0, slot], col)]
            where = jnp.where(slot < count, cols_ref[0, slot], -1)
            wide.append(
                jnp.concatenate(
                    [jnp.where(where == b, piece, jnp.zeros_like(piece)) for b in range(SIDE)], axis=0
                )
            )
        left = jnp.concatenate(wide, axis=1)
        right = vals[pl.ds(first, RUN)].reshape(RUN * BLOCK, BLOCK)
        return total + jnp.dot(left, right, preferred_element_type=F32)

    sums = lax.fori_loop(0, SLOTS // RUN, one_run, jnp.zeros((SIDE * ROWS, BLOCK), F32)).astype(BF)
    out = jnp.zeros((ROWS, NODES), F32)
    for block in range(SIDE):
        out = out + lax.dot_general(
            sums[block * ROWS : (block + 1) * ROWS, :],
            hot[:, block * BLOCK : (block + 1) * BLOCK],
            NT,
            preferred_element_type=F32,
        )
    gf_ref[...] = out.astype(BF)

    r_wait(3, whole, y_peer, (y_peer(1) * SIDE + h, feat))
    gw_ref[...] = whole[...]

    for turn in range(4):
        for step in range(1, SIDE):
            if turn in FAR_FIRST[4 - WINDOW :]:
                a_copy(turn, step).wait_send()
            d_copy(turn, step).wait_send()

    def r_done(step, _):
        r_h(step).wait_send()
        r_f(step).wait_send()
        r_y(step).wait_send()
        r_all(step).wait_send()
        return 0

    lax.fori_loop(1, SIDE, r_done, 0)

    def pairs_done(i, _):
        @pl.when(jnp.logical_not(b_here(i)))
        def _():
            b_copy(i).wait_send()

        @pl.when(jnp.logical_not(c_here(i)))
        def _():
            c_copy(i).wait_send()

        return 0

    lax.fori_loop(0, 2 * SIDE, pairs_done, 0)


def write_kernel(*refs):
    sources, targets, sems = refs[:4], refs[4:8], refs[8]
    copies = [
        pltpu.make_async_copy(source, target, sems.at[i])
        for i, (source, target) in enumerate(zip(sources, targets))
    ]
    for copy in copies:
        copy.start()
    for copy in copies:
        copy.wait()


def per_device(
    features_t,
    node_order,
    tile_rows,
    tile_cols,
    tile_vals,
    tile_count,
    weight,
    bias_term,
    cotangent,
):
    vmem = pl.BlockSpec(memory_space=pltpu.VMEM)
    hbm = pl.BlockSpec(memory_space=pl.ANY)
    operands = (
        tile_rows,
        tile_cols,
        tile_count,
        node_order.reshape(1, NODES),
        features_t,
        tile_vals.reshape(SLOTS, BLOCK, BLOCK),
        weight,
        bias_term.reshape(1, HID),
        cotangent,
    )
    operands = [
        pltpu.with_memory_space_constraint(operand, pltpu.HBM) if operand.size > 1 else operand
        for operand in operands
    ]
    dma = pltpu.SemaphoreType.DMA
    shapes = (((HID, BLOCK), BF), ((SIDE, ROWS, HID), F32), ((1, HID), F32), ((ROWS, NODES), BF))
    made = pl.pallas_call(
        exchange_kernel,
        out_shape=tuple(pltpu.VMEM(*shape) for shape in shapes),
        in_specs=[hbm] * 9,
        out_specs=(vmem,) * 4,
        scratch_shapes=[
            pltpu.SMEM((1, SLOTS), jnp.int32),
            pltpu.SMEM((1, SLOTS), jnp.int32),
            pltpu.SMEM((1,), jnp.int32),
            pltpu.VMEM((1, SLOTS), jnp.int32),
            pltpu.VMEM((1, NODES), jnp.int32),
            pltpu.VMEM((ROWS, NODES), BF),
            pltpu.VMEM((SLOTS, BLOCK, BLOCK), BF),
            pltpu.VMEM((F_IN, HID), BF),
            pltpu.VMEM((1, HID), F32),
            pltpu.VMEM((HID, BLOCK), BF),
            pltpu.VMEM((NODES, NODES), BF),
            pltpu.VMEM((SIDE, ROWS, BLOCK), BF),
            pltpu.VMEM((SLOTS * ROWS, BLOCK), F32),
            pltpu.VMEM((PAIRS * ROWS, BLOCK), F32),
            pltpu.VMEM((PAIRS, ROWS, BLOCK), BF),
            pltpu.VMEM((SIDE, 2 * SIDE, ROWS, BLOCK), BF),
            pltpu.VMEM((2 * SIDE, ROWS, BLOCK), BF),
            pltpu.VMEM((2 * SIDE, ROWS, BLOCK), BF),
            pltpu.VMEM((F_IN, BLOCK), BF),
            pltpu.VMEM((SIDE, ROWS, BLOCK), BF),
            pltpu.VMEM((PAIRS, ROWS, BLOCK), BF),
            pltpu.VMEM((SIDE, 2 * ROWS + 8, BLOCK), F32),
            pltpu.VMEM((SIDE, 2 * ROWS + 8, BLOCK), F32),
            pltpu.VMEM((SIDE, 2 * ROWS + 8, BLOCK), F32),
            pltpu.VMEM((SIDE, 2 * ROWS + 8, BLOCK), F32),
            pltpu.VMEM((SIDE, ROWS, HID), F32),
            dma((9,)),
            dma((SLOTS // RUN,)),
            dma((4, SIDE)),
            dma((4, SIDE)),
            dma((2 * SIDE,)),
            dma((2 * SIDE,)),
            dma((2 * SIDE,)),
            dma((2 * SIDE,)),
            dma((4, SIDE)),
            dma((4, SIDE)),
            dma((4, SIDE)),
            dma((4, SIDE)),
        ],
        compiler_params=pltpu.CompilerParams(
            collective_id=0, has_side_effects=True, vmem_limit_bytes=VMEM_BYTES
        ),
        name="exchange_layer",
    )(*operands)
    act, grad_w, grad_b, grad_f = pl.pallas_call(
        write_kernel,
        out_shape=tuple(jax.ShapeDtypeStruct(*shape) for shape in shapes),
        in_specs=[vmem] * 4,
        out_specs=(hbm,) * 4,
        scratch_shapes=[dma((4,))],
        name="write_outputs",
    )(*made)
    return act, grad_w.reshape(F_IN, HID), grad_b.reshape(HID), grad_f


def solution(mesh):
    return jax.shard_map(
        per_device,
        mesh=mesh,
        in_specs=(
            P("feat", "col"),
            P("col"),
            P("col", None),
            P("col", None),
            P("col", None, None, None),
            P("col"),
            P(),
            P(),
            P(None, ("col", "feat")),
        ),
        out_specs=(P(None, ("col", "feat")), P(), P(), P("feat", "col")),
        check_vma=False,
    )
```

```python
import jax
import jax.numpy as jnp
from jax import lax
from jax.experimental import pallas as pl
from jax.experimental.pallas import tpu as pltpu
from jax.sharding import PartitionSpec as P

BF = jnp.bfloat16
F32 = jnp.float32
MESH = pl.DeviceIdType.MESH
NT = (((1,), (1,)), ((), ()))

BLOCK = 128
ROWS = 16
SLOTS = 96
RUN = 12
SIDE = 8
PAIRS = 128
HID = 256
F_IN = 128
NODES = 1024
VMEM_BYTES = 40 << 20
STEPS = (4, 3, 5, 2, 6, 1, 7)
FAR_FIRST = (2, 1, 3, 0)
NEAR_FIRST = (0, 1, 3, 2)


def pair_of(row, group):
    return (row >> 3) * 2 + jnp.minimum((row - group) & 7, 1)


def one_hot(order_row):
    node = lax.broadcasted_iota(jnp.int32, (NODES, order_row.shape[1]), 0)
    return jnp.where(node == order_row, 1.0, 0.0).astype(BF)


def exchange_kernel(
    rows_hbm,
    cols_hbm,
    count_hbm,
    order_hbm,
    feats_hbm,
    vals_hbm,
    weight_hbm,
    bias_hbm,
    cot_hbm,
    act_ref,
    gw_ref,
    gb_ref,
    gf_ref,
    rows_ref,
    cols_ref,
    count_ref,
    rows_wide,
    order_ref,
    feats_ref,
    vals,
    weight_ref,
    bias_ref,
    cot_ref,
    hot,
    perm,
    products,
    totals,
    part,
    from_y,
    sum_y,
    pieces,
    agg,
    grad_out,
    gath,
    terms,
    red_y,
    red_xc,
    red_z,
    whole,
    in_sem,
    vals_sem,
    a_send,
    a_recv,
    b_send,
    b_recv,
    c_send,
    c_recv,
    d_send,
    d_recv,
    r_send,
    r_recv,
):
    col = lax.axis_index("col")
    feat = lax.axis_index("feat")
    y = col // SIDE
    h = col % SIDE
    z = h // 2

    def vals_copy(run):
        at = pl.ds(run * RUN, RUN)
        return pltpu.make_async_copy(vals_hbm.at[at], vals.at[at], vals_sem.at[run])

    inputs = [
        pltpu.make_async_copy(src, dst, in_sem.at[i])
        for i, (src, dst) in enumerate(
            (
                (order_hbm, order_ref),
                (feats_hbm, feats_ref),
                (rows_hbm, rows_ref),
                (cols_hbm, cols_ref),
                (rows_hbm, rows_wide),
                (count_hbm, count_ref),
                (weight_hbm, weight_ref),
                (bias_hbm, bias_ref),
                (cot_hbm, cot_ref),
            )
        )
    ]
    for copy in inputs[:6]:
        copy.start()
    for run in range(SLOTS // RUN):
        vals_copy(run).start()
    for copy in inputs[6:]:
        copy.start()

    x, z_lo, core = feat // 2, feat % 2, h % 2
    place_xc, place_z = x * 2 + core, z * 2 + z_lo
    y_peer, y_device, xc_peer, xc_device, z_peer, z_device = ([None] for _ in range(6))
    for step in range(1, SIDE):
        y_peer.append(lax.rem(y + step, SIDE))
        y_device.append((y_peer[step] * SIDE + h, feat))
        place = lax.rem(place_xc + step, SIDE)
        xc_peer.append(place)
        xc_device.append((y * SIDE + z * 2 + place % 2, place // 2 * 2 + z_lo))
        place = lax.rem(place_z + step, SIDE)
        z_peer.append(place)
        z_device.append((y * SIDE + place // 2 * 2 + core, x * 2 + place % 2))
    holder = (h, lax.rem(h + 1, SIDE))
    namer = (feat, lax.rem(feat + SIDE - 1, SIDE))
    is_self = (feat == holder[0], feat == holder[1])

    barrier = pltpu.get_barrier_semaphore()

    def greet(device):
        pl.semaphore_signal(barrier, inc=1, device_id=device, device_id_type=MESH)

    for other in range(SIDE):
        for q in range(2):

            @pl.when(jnp.logical_not(jnp.logical_and(is_self[q], other == h)))
            def _(other=other, q=q):
                greet((y * SIDE + other, holder[q]))

            @pl.when(jnp.logical_not(jnp.logical_and(is_self[q], other == feat)))
            def _(other=other, q=q):
                greet((y * SIDE + namer[q], other))

    for step in STEPS:
        greet(z_device[step])
        greet(y_device[step])
        greet(xc_device[step])

    inputs[0].wait()
    inputs[1].wait()
    order = order_ref[...] - col * NODES
    feats = feats_ref[...]
    for block in range(SIDE):
        at = slice(block * BLOCK, (block + 1) * BLOCK)
        hot[:, at] = one_hot(order[:, at])
        perm[block] = jnp.dot(feats, hot[:, at], preferred_element_type=F32).astype(BF)

    for copy in inputs[2:6]:
        copy.wait()
    count = count_ref[0]

    def one_forward(run, _):
        vals_copy(run).wait()
        for step in range(RUN):
            slot = run * RUN + step
            products[pl.ds(pl.multiple_of(slot * ROWS, ROWS), ROWS), :] = lax.dot_general(
                perm[cols_ref[0, slot]], vals[slot], NT, preferred_element_type=F32
            )
        return 0

    lax.fori_loop(0, SLOTS // RUN, one_forward, 0)
    place = pair_of(rows_wide[...], col)
    place = jnp.where(lax.broadcasted_iota(jnp.int32, (1, SLOTS), 1) < count, place, -1)
    pick = jnp.where(lax.broadcasted_iota(jnp.int32, (PAIRS, SLOTS), 0) == place, 1.0, 0.0).astype(BF)
    for f in range(ROWS):
        value = products[pl.ds(f, SLOTS, stride=ROWS), :]
        high = value.astype(BF)
        low = (value - high.astype(F32)).astype(BF)
        totals[pl.ds(f, PAIRS, stride=ROWS), :] = jnp.dot(
            pick, high, preferred_element_type=F32
        ) + jnp.dot(pick, low, preferred_element_type=F32)
    part[...] = totals[...].reshape(PAIRS, ROWS, BLOCK).astype(BF)

    for copy in inputs[6:]:
        copy.wait()
    weight = weight_ref[...]
    weight_t = weight.T
    bias = jnp.broadcast_to(bias_ref[...], (8, HID)).T[:, :1]

    selves = jnp.where(is_self[0], 1, 0) + jnp.where(is_self[1], 1, 0)
    pl.semaphore_wait(barrier, 3 * (SIDE - 1) + 4 * SIDE - 2 * selves)

    def a_copy(turn, step):
        at = (z + turn) % 4 * 4
        return pltpu.make_async_remote_copy(
            src_ref=part.at[pl.ds(y_peer[step] * 2 * SIDE + at, 4)],
            dst_ref=from_y.at[step, pl.ds(at, 4)],
            send_sem=a_send.at[turn, step],
            recv_sem=a_recv.at[turn, step],
            device_id=y_device[step],
            device_id_type=MESH,
        )

    for turn in FAR_FIRST:
        for step in STEPS:
            a_copy(turn, step).start()

    def b_copy(other, q):
        return pltpu.make_async_remote_copy(
            src_ref=sum_y.at[other * 2 + q],
            dst_ref=pieces.at[q * SIDE + feat],
            send_sem=b_send.at[other * 2 + q],
            recv_sem=b_recv.at[q * SIDE + feat],
            device_id=(y * SIDE + other, holder[q]),
            device_id_type=MESH,
        )

    for turn in FAR_FIRST:
        for step in range(1, SIDE):
            a_copy(turn, step).wait_recv()
        for k in range(4):
            other, q = (z + turn) % 4 * 2 + k // 2, k % 2
            i = other * 2 + q
            total = part[y * 2 * SIDE + i].astype(F32)
            for step in range(1, SIDE):
                total = total + from_y[step, i].astype(F32)
            sum_y[i] = total.astype(BF)
            here = jnp.logical_and(is_self[q], other == h)

            @pl.when(here)
            def _(i=i, q=q):
                pieces[q * SIDE + feat] = sum_y[i]

            @pl.when(jnp.logical_not(here))
            def _(other=other, q=q):
                b_copy(other, q).start()

    for q in range(2):
        for source in range(SIDE):

            @pl.when(jnp.logical_not(jnp.logical_and(is_self[q], source == feat)))
            def _(q=q, source=source):
                pltpu.make_async_remote_copy(
                    src_ref=sum_y.at[0],
                    dst_ref=pieces.at[q * SIDE + source],
                    send_sem=b_send.at[0],
                    recv_sem=b_recv.at[q * SIDE + source],
                    device_id=(y * SIDE + namer[q], source),
                    device_id_type=MESH,
                ).wait_recv()

    for i in range(SIDE):
        both = pieces[i].astype(F32) + pieces[SIDE + i].astype(F32)
        agg[i * ROWS : (i + 1) * ROWS, :] = both.astype(BF)

    aggregated = agg[...]
    pre = jnp.dot(weight_t, aggregated, preferred_element_type=F32) + bias
    root = 0.7978845608028654
    square = pre * pre
    bend = jnp.tanh(root * (pre + 0.044715 * (square * pre)))
    half = 0.5 * (1.0 + bend)
    act_ref[...] = (pre * half).astype(BF)
    slope = half + 0.5 * pre * (1.0 - bend * bend) * (root * (1.0 + 3.0 * 0.044715 * square))
    grad_pre = (cot_ref[...].astype(F32) * slope).astype(BF)
    grad_agg = jnp.dot(weight, grad_pre, preferred_element_type=F32).astype(BF)
    for i in range(SIDE):
        grad_out[i] = grad_agg[i * ROWS : (i + 1) * ROWS, :]

    def c_copy(other, q):
        return pltpu.make_async_remote_copy(
            src_ref=grad_out.at[other],
            dst_ref=gath.at[y * 2 * SIDE + h * 2 + q],
            send_sem=c_send.at[other * 2 + q],
            recv_sem=c_recv.at[h * 2 + q],
            device_id=(y * SIDE + namer[q], other),
            device_id_type=MESH,
        )

    for other in range(SIDE):
        for q in range(2):
            here = jnp.logical_and(is_self[q], other == feat)

            @pl.when(here)
            def _(other=other, q=q):
                gath[y * 2 * SIDE + h * 2 + q] = grad_out[other]

            @pl.when(jnp.logical_not(here))
            def _(other=other, q=q):
                c_copy(other, q).start()

    grad_w = lax.dot_general(aggregated, grad_pre, NT, preferred_element_type=F32)
    grad_b = lax.dot_general(jnp.ones((ROWS, BLOCK), BF), grad_pre, NT, preferred_element_type=F32)
    upper = lax.broadcasted_iota(jnp.int32, (ROWS, BLOCK), 0) < 8
    grad_b = jnp.where(upper, grad_b[:, :BLOCK], grad_b[:, BLOCK:]).astype(BF)
    grad_w = grad_w.astype(BF)
    for i in range(SIDE):
        for half in range(2):
            at = slice(half * BLOCK, (half + 1) * BLOCK)
            terms[i, half * ROWS : (half + 1) * ROWS, :] = grad_w[i * ROWS : (i + 1) * ROWS, at]
        terms[i, 2 * ROWS :, :] = grad_b

    def r_copy(stage, step, src, dst, device):
        return pltpu.make_async_remote_copy(
            src_ref=src,
            dst_ref=dst,
            send_sem=r_send.at[stage, step],
            recv_sem=r_recv.at[stage, step],
            device_id=device,
            device_id_type=MESH,
        )

    def r_y(step):
        return r_copy(0, step, terms.at[y_peer[step]], red_y.at[y], y_device[step])

    def r_xc(step):
        return r_copy(1, step, red_xc.at[place_xc], red_xc.at[place_xc], xc_device[step])

    def r_z(step):
        return r_copy(2, step, red_z.at[place_z], red_z.at[place_z], z_device[step])

    def r_all(step):
        return r_copy(3, step, whole.at[y], whole.at[y], y_device[step])

    def r_start(make):
        for step in STEPS:
            make(step).start()

    def r_wait(stage, buffer, peer, device):
        for step in range(1, SIDE):
            r_copy(stage, step, buffer.at[0], buffer.at[peer[SIDE - step]], device[1]).wait_recv()

    def r_sent(make):
        for step in range(1, SIDE):
            make(step).wait_send()

    r_start(r_y)

    def c_wait(other, q):
        @pl.when(jnp.logical_not(jnp.logical_and(is_self[q], other == h)))
        def _():
            pltpu.make_async_remote_copy(
                src_ref=grad_out.at[0],
                dst_ref=gath.at[y * 2 * SIDE + other * 2 + q],
                send_sem=c_send.at[0],
                recv_sem=c_recv.at[other * 2 + q],
                device_id=(y * SIDE + other, holder[q]),
                device_id_type=MESH,
            ).wait_recv()

    def d_copy(turn, step):
        own = gath.at[pl.ds(y * 2 * SIDE + (z + turn) % 4 * 4, 4)]
        return pltpu.make_async_remote_copy(
            src_ref=own,
            dst_ref=own,
            send_sem=d_send.at[turn, step],
            recv_sem=d_recv.at[turn, step],
            device_id=y_device[step],
            device_id_type=MESH,
        )

    for turn in NEAR_FIRST:
        for k in range(4):
            c_wait((z + turn) % 4 * 2 + k // 2, k % 2)
        for step in STEPS:
            d_copy(turn, step).start()

    def total_of(buffer):
        total = buffer[0].astype(F32)
        for i in range(1, SIDE):
            total = total + buffer[i].astype(F32)
        return total

    red_y[y] = terms[y]
    r_wait(0, red_y, y_peer, y_device)
    red_xc[place_xc] = total_of(red_y).astype(BF)
    r_start(r_xc)
    for turn in range(4):
        for step in range(1, SIDE):
            a_copy(turn, step).wait_send()
    r_sent(r_y)
    r_wait(1, red_xc, xc_peer, xc_device)
    red_z[place_z] = total_of(red_xc).astype(BF)
    r_start(r_z)
    for other in range(SIDE):
        for q in range(2):

            @pl.when(jnp.logical_not(jnp.logical_and(is_self[q], other == h)))
            def _(other=other, q=q):
                b_copy(other, q).wait_send()

            @pl.when(jnp.logical_not(jnp.logical_and(is_self[q], other == feat)))
            def _(other=other, q=q):
                c_copy(other, q).wait_send()

    r_sent(r_xc)
    r_wait(2, red_z, z_peer, z_device)
    final = total_of(red_z)
    for half in range(2):
        at = slice(half * BLOCK, (half + 1) * BLOCK)
        whole[y, :, at] = final[half * ROWS : (half + 1) * ROWS, :]
        gb_ref[:, at] = final[2 * ROWS + 8 * half : 2 * ROWS + 8 * half + 1, :]
    r_start(r_all)

    for turn in NEAR_FIRST:
        for step in range(1, SIDE):
            pltpu.make_async_remote_copy(
                src_ref=gath.at[pl.ds(0, 4)],
                dst_ref=gath.at[pl.ds(y_peer[SIDE - step] * 2 * SIDE + (z + turn) % 4 * 4, 4)],
                send_sem=d_send.at[turn, step],
                recv_sem=d_recv.at[turn, step],
                device_id=y_device[1],
                device_id_type=MESH,
            ).wait_recv()

    def one_run(run, total):
        first = run * RUN
        wide = []
        for step in range(RUN):
            slot = first + step
            piece = gath[pair_of(rows_ref[0, slot], col)]
            where = jnp.where(slot < count, cols_ref[0, slot], -1)
            wide.append(
                jnp.concatenate(
                    [jnp.where(where == b, piece, jnp.zeros_like(piece)) for b in range(SIDE)], axis=0
                )
            )
        left = jnp.concatenate(wide, axis=1)
        right = vals[pl.ds(first, RUN)].reshape(RUN * BLOCK, BLOCK)
        return total + jnp.dot(left, right, preferred_element_type=F32)

    sums = lax.fori_loop(0, SLOTS // RUN, one_run, jnp.zeros((SIDE * ROWS, BLOCK), F32)).astype(BF)
    out = jnp.zeros((ROWS, NODES), F32)
    for block in range(SIDE):
        out = out + lax.dot_general(
            sums[block * ROWS : (block + 1) * ROWS, :],
            hot[:, block * BLOCK : (block + 1) * BLOCK],
            NT,
            preferred_element_type=F32,
        )
    gf_ref[...] = out.astype(BF)

    for turn in range(4):
        for step in range(1, SIDE):
            d_copy(turn, step).wait_send()
    r_sent(r_z)
    r_wait(3, whole, y_peer, y_device)
    gw_ref[...] = whole[...]
    r_sent(r_all)


def write_kernel(*refs):
    sources, targets, sems = refs[:4], refs[4:8], refs[8]
    copies = [
        pltpu.make_async_copy(source, target, sems.at[i])
        for i, (source, target) in enumerate(zip(sources, targets))
    ]
    for copy in copies:
        copy.start()
    for copy in copies:
        copy.wait()


def per_device(
    features_t,
    node_order,
    tile_rows,
    tile_cols,
    tile_vals,
    tile_count,
    weight,
    bias_term,
    cotangent,
):
    vmem = pl.BlockSpec(memory_space=pltpu.VMEM)
    hbm = pl.BlockSpec(memory_space=pl.ANY)
    operands = (
        tile_rows,
        tile_cols,
        tile_count,
        node_order.reshape(1, NODES),
        features_t,
        tile_vals.reshape(SLOTS, BLOCK, BLOCK),
        weight,
        bias_term.reshape(1, HID),
        cotangent,
    )
    operands = [
        pltpu.with_memory_space_constraint(operand, pltpu.HBM) if operand.size > 1 else operand
        for operand in operands
    ]
    dma = pltpu.SemaphoreType.DMA
    shapes = (((HID, BLOCK), BF), ((SIDE, ROWS, HID), F32), ((1, HID), F32), ((ROWS, NODES), BF))
    made = pl.pallas_call(
        exchange_kernel,
        out_shape=tuple(pltpu.VMEM(*shape) for shape in shapes),
        in_specs=[hbm] * 9,
        out_specs=(vmem,) * 4,
        scratch_shapes=[
            pltpu.SMEM((1, SLOTS), jnp.int32),
            pltpu.SMEM((1, SLOTS), jnp.int32),
            pltpu.SMEM((1,), jnp.int32),
            pltpu.VMEM((1, SLOTS), jnp.int32),
            pltpu.VMEM((1, NODES), jnp.int32),
            pltpu.VMEM((ROWS, NODES), BF),
            pltpu.VMEM((SLOTS, BLOCK, BLOCK), BF),
            pltpu.VMEM((F_IN, HID), BF),
            pltpu.VMEM((1, HID), F32),
            pltpu.VMEM((HID, BLOCK), BF),
            pltpu.VMEM((NODES, NODES), BF),
            pltpu.VMEM((SIDE, ROWS, BLOCK), BF),
            pltpu.VMEM((SLOTS * ROWS, BLOCK), F32),
            pltpu.VMEM((PAIRS * ROWS, BLOCK), F32),
            pltpu.VMEM((PAIRS, ROWS, BLOCK), BF),
            pltpu.VMEM((SIDE, 2 * SIDE, ROWS, BLOCK), BF),
            pltpu.VMEM((2 * SIDE, ROWS, BLOCK), BF),
            pltpu.VMEM((2 * SIDE, ROWS, BLOCK), BF),
            pltpu.VMEM((F_IN, BLOCK), BF),
            pltpu.VMEM((SIDE, ROWS, BLOCK), BF),
            pltpu.VMEM((PAIRS, ROWS, BLOCK), BF),
            pltpu.VMEM((SIDE, 3 * ROWS, BLOCK), BF),
            pltpu.VMEM((SIDE, 3 * ROWS, BLOCK), BF),
            pltpu.VMEM((SIDE, 3 * ROWS, BLOCK), BF),
            pltpu.VMEM((SIDE, 3 * ROWS, BLOCK), BF),
            pltpu.VMEM((SIDE, ROWS, HID), F32),
            dma((9,)),
            dma((SLOTS // RUN,)),
            dma((4, SIDE)),
            dma((4, SIDE)),
            dma((2 * SIDE,)),
            dma((2 * SIDE,)),
            dma((2 * SIDE,)),
            dma((2 * SIDE,)),
            dma((4, SIDE)),
            dma((4, SIDE)),
            dma((4, SIDE)),
            dma((4, SIDE)),
        ],
        compiler_params=pltpu.CompilerParams(
            collective_id=0, has_side_effects=True, vmem_limit_bytes=VMEM_BYTES
        ),
        name="exchange_layer",
    )(*operands)
    act, grad_w, grad_b, grad_f = pl.pallas_call(
        write_kernel,
        out_shape=tuple(jax.ShapeDtypeStruct(*shape) for shape in shapes),
        in_specs=[vmem] * 4,
        out_specs=(hbm,) * 4,
        scratch_shapes=[dma((4,))],
        compiler_params=pltpu.CompilerParams(vmem_limit_bytes=4 << 20),
        name="write_outputs",
    )(*made)
    return act, grad_w.reshape(F_IN, HID), grad_b.reshape(HID), grad_f


def solution(mesh):
    return jax.shard_map(
        per_device,
        mesh=mesh,
        in_specs=(
            P("feat", "col"),
            P("col"),
            P("col", None),
            P("col", None),
            P("col", None, None, None),
            P("col"),
            P(),
            P(),
            P(None, ("col", "feat")),
        ),
        out_specs=(P(None, ("col", "feat")), P(), P(), P("feat", "col")),
        check_vma=False,
    )
```

```python
import jax
import jax.numpy as jnp
from jax import lax
from jax.experimental import pallas as pl
from jax.experimental.pallas import tpu as pltpu
from jax.sharding import PartitionSpec as P

BF = jnp.bfloat16
F32 = jnp.float32
MESH = pl.DeviceIdType.MESH
NT = (((1,), (1,)), ((), ()))

BLOCK = 128
ROWS = 16
SLOTS = 96
RUN = 12
SIDE = 8
PAIRS = 128
HID = 256
F_IN = 128
NODES = 1024
VMEM_BYTES = 40 << 20
STEPS = (4, 3, 5, 2, 6, 1, 7)
MINE = 12
NEAR_FIRST = (0, 1, 3, 2)


def pair_of(row, group):
    return (row >> 3) * 2 + jnp.minimum((row - group) & 7, 1)


def one_hot(order_row):
    node = lax.broadcasted_iota(jnp.int32, (NODES, order_row.shape[1]), 0)
    return jnp.where(node == order_row, 1.0, 0.0).astype(BF)


def exchange_kernel(
    rows_hbm,
    cols_hbm,
    count_hbm,
    order_hbm,
    feats_hbm,
    vals_hbm,
    weight_hbm,
    bias_hbm,
    cot_hbm,
    act_ref,
    gw_ref,
    gb_ref,
    gf_ref,
    rows_ref,
    cols_ref,
    count_ref,
    rows_wide,
    order_ref,
    feats_ref,
    vals,
    weight_ref,
    bias_ref,
    cot_ref,
    hot,
    perm,
    products,
    totals,
    part,
    core_in,
    from_y,
    sum_y,
    pieces,
    agg,
    grad_out,
    gath,
    terms,
    red_y,
    red_xc,
    red_z,
    whole,
    in_sem,
    vals_sem,
    core_send,
    core_recv,
    a_send,
    a_recv,
    b_send,
    b_recv,
    c_send,
    c_recv,
    d_send,
    d_recv,
    r_send,
    r_recv,
):
    col = lax.axis_index("col")
    feat = lax.axis_index("feat")
    y = col // SIDE
    h = col % SIDE
    z = h // 2

    def vals_copy(run):
        at = pl.ds(run * RUN, RUN)
        return pltpu.make_async_copy(vals_hbm.at[at], vals.at[at], vals_sem.at[run])

    inputs = [
        pltpu.make_async_copy(src, dst, in_sem.at[i])
        for i, (src, dst) in enumerate(
            (
                (order_hbm, order_ref),
                (feats_hbm, feats_ref),
                (rows_hbm, rows_ref),
                (cols_hbm, cols_ref),
                (rows_hbm, rows_wide),
                (count_hbm, count_ref),
                (weight_hbm, weight_ref),
                (bias_hbm, bias_ref),
                (cot_hbm, cot_ref),
            )
        )
    ]
    for copy in inputs[:6]:
        copy.start()
    for run in range(SLOTS // RUN):
        vals_copy(run).start()
    for copy in inputs[6:]:
        copy.start()

    x, z_lo, core = feat // 2, feat % 2, h % 2
    place_xc, place_z = x * 2 + core, z * 2 + z_lo
    y_peer, y_device, xc_peer, xc_device, z_peer, z_device = ([None] for _ in range(6))
    for step in range(1, SIDE):
        y_peer.append(lax.rem(y + step, SIDE))
        y_device.append((y_peer[step] * SIDE + h, feat))
        place = lax.rem(place_xc + step, SIDE)
        xc_peer.append(place)
        xc_device.append((y * SIDE + z * 2 + place % 2, place // 2 * 2 + z_lo))
        place = lax.rem(place_z + step, SIDE)
        z_peer.append(place)
        z_device.append((y * SIDE + place // 2 * 2 + core, x * 2 + place % 2))
    holder = (h, lax.rem(h + 1, SIDE))
    namer = (feat, lax.rem(feat + SIDE - 1, SIDE))
    is_self = (feat == holder[0], feat == holder[1])

    barrier = pltpu.get_barrier_semaphore()

    def greet(device):
        pl.semaphore_signal(barrier, inc=1, device_id=device, device_id_type=MESH)

    for other in range(SIDE):
        for q in range(2):

            @pl.when(jnp.logical_not(jnp.logical_and(is_self[q], other == h)))
            def _(other=other, q=q):
                greet((y * SIDE + other, holder[q]))

            @pl.when(jnp.logical_not(jnp.logical_and(is_self[q], other == feat)))
            def _(other=other, q=q):
                greet((y * SIDE + namer[q], other))

    for step in STEPS:
        greet(z_device[step])
        greet(y_device[step])
        greet(xc_device[step])

    inputs[0].wait()
    inputs[1].wait()
    order = order_ref[...] - col * NODES
    feats = feats_ref[...]
    for block in range(SIDE):
        at = slice(block * BLOCK, (block + 1) * BLOCK)
        hot[:, at] = one_hot(order[:, at])
        perm[block] = jnp.dot(feats, hot[:, at], preferred_element_type=F32).astype(BF)

    for copy in inputs[2:6]:
        copy.wait()
    count = count_ref[0]

    def one_forward(run, _):
        vals_copy(run).wait()
        for step in range(RUN):
            slot = run * RUN + step
            products[pl.ds(pl.multiple_of(slot * ROWS, ROWS), ROWS), :] = lax.dot_general(
                perm[cols_ref[0, slot]], vals[slot], NT, preferred_element_type=F32
            )
        return 0

    lax.fori_loop(0, SLOTS // RUN, one_forward, 0)
    row_block = rows_wide[...]
    owner_h = (row_block >> 3) & 7
    second = jnp.minimum((row_block - col) & 7, 1)
    theirs = jnp.where((owner_h & 1) == core, 0, 4)
    place = jnp.where(second == core, owner_h, 8 + (owner_h >> 1) + theirs)
    place = (row_block >> 6) * 2 * SIDE + place
    place = jnp.where(lax.broadcasted_iota(jnp.int32, (1, SLOTS), 1) < count, place, -1)
    pick = jnp.where(lax.broadcasted_iota(jnp.int32, (PAIRS, SLOTS), 0) == place, 1.0, 0.0).astype(BF)
    for f in range(ROWS):
        value = products[pl.ds(f, SLOTS, stride=ROWS), :]
        high = value.astype(BF)
        low = (value - high.astype(F32)).astype(BF)
        totals[pl.ds(f, PAIRS, stride=ROWS), :] = jnp.dot(
            pick, high, preferred_element_type=F32
        ) + jnp.dot(pick, low, preferred_element_type=F32)
    part[...] = totals[...].reshape(SIDE, 2 * SIDE, ROWS, BLOCK).astype(BF)

    for copy in inputs[6:]:
        copy.wait()
    weight = weight_ref[...]
    weight_t = weight.T
    bias = jnp.broadcast_to(bias_ref[...], (8, HID)).T[:, :1]

    selves = jnp.where(is_self[0], 1, 0) + jnp.where(is_self[1], 1, 0)
    pl.semaphore_wait(barrier, 3 * (SIDE - 1) + 4 * SIDE - 2 * selves)

    core_copy = pltpu.make_async_remote_copy(
        src_ref=part.at[:, pl.ds(MINE, 4)],
        dst_ref=core_in,
        send_sem=core_send,
        recv_sem=core_recv,
        device_id=(y * SIDE + z * 2 + 1 - core, feat),
        device_id_type=MESH,
    )
    core_copy.start()

    def a_copy(which, step):
        at = pl.ds(0, SIDE) if which == 0 else pl.ds(SIDE, 4)
        return pltpu.make_async_remote_copy(
            src_ref=part.at[y_peer[step], at],
            dst_ref=from_y.at[step, at],
            send_sem=a_send.at[which, step],
            recv_sem=a_recv.at[which, step],
            device_id=y_device[step],
            device_id_type=MESH,
        )

    for step in STEPS:
        a_copy(0, step).start()
    core_copy.wait_recv()
    for i in range(SIDE):
        at = (i * 2 * SIDE + SIDE) * ROWS
        own = totals[at : at + 4 * ROWS, :].reshape(4, ROWS, BLOCK)
        part[i, SIDE:MINE] = (own + core_in[i].astype(F32)).astype(BF)
    for step in STEPS:
        a_copy(1, step).start()

    own_block = jnp.where(core == 0, holder[0], holder[1])
    shared_block = z * 2 + 1
    far_first = [lax.rem(z + turn, 4) for turn in (2, 1, 3, 0)]
    b_own = [(i * 2 + k, i * 2 + k, own_block, core * SIDE + feat) for i in far_first for k in range(2)]
    b_shared = [(SIDE + i, i * 2 + core, shared_block, feat) for i in far_first]
    b_parts = b_own + b_shared

    def b_here(part_of):
        return jnp.logical_and(part_of[1] == h, part_of[2] == feat)

    def b_copy(part_of):
        i, other, block, slot = part_of
        return pltpu.make_async_remote_copy(
            src_ref=sum_y.at[i],
            dst_ref=pieces.at[slot],
            send_sem=b_send.at[i],
            recv_sem=b_recv.at[slot],
            device_id=(y * SIDE + other, block),
            device_id_type=MESH,
        )

    for which, parts_of in enumerate((b_own, b_shared)):
        for step in range(1, SIDE):
            a_copy(which, step).wait_recv()
        for part_of in parts_of:
            i = part_of[0]
            total = part[y, i].astype(F32)
            for step in range(1, SIDE):
                total = total + from_y[step, i].astype(F32)
            sum_y[i] = total.astype(BF)

            @pl.when(b_here(part_of))
            def _(part_of=part_of):
                pieces[part_of[3]] = sum_y[part_of[0]]

            @pl.when(jnp.logical_not(b_here(part_of)))
            def _(part_of=part_of):
                b_copy(part_of).start()

    even = feat % 2 == 0
    first_from = jnp.where(even, feat, feat - 1 + core)

    def b_wait(slot, source_h, source_feat):
        @pl.when(jnp.logical_not(jnp.logical_and(source_h == h, source_feat == feat)))
        def _():
            pltpu.make_async_remote_copy(
                src_ref=sum_y.at[0],
                dst_ref=pieces.at[slot],
                send_sem=b_send.at[0],
                recv_sem=b_recv.at[slot],
                device_id=(y * SIDE + source_h, source_feat),
                device_id_type=MESH,
            ).wait_recv()

    for source in range(SIDE):
        b_wait(source, first_from, source)

    @pl.when(even)
    def _():
        for source in range(SIDE):
            b_wait(SIDE + source, namer[1], source)

    @pl.when(jnp.logical_not(even))
    def _():
        pieces[SIDE:] = jnp.zeros((SIDE, ROWS, BLOCK), BF)

    for i in range(SIDE):
        both = pieces[i].astype(F32) + pieces[SIDE + i].astype(F32)
        agg[i * ROWS : (i + 1) * ROWS, :] = both.astype(BF)

    aggregated = agg[...]
    pre = jnp.dot(weight_t, aggregated, preferred_element_type=F32) + bias
    root = 0.7978845608028654
    square = pre * pre
    bend = jnp.tanh(root * (pre + 0.044715 * (square * pre)))
    half = 0.5 * (1.0 + bend)
    act_ref[...] = (pre * half).astype(BF)
    slope = half + 0.5 * pre * (1.0 - bend * bend) * (root * (1.0 + 3.0 * 0.044715 * square))
    grad_pre = (cot_ref[...].astype(F32) * slope).astype(BF)
    grad_agg = jnp.dot(weight, grad_pre, preferred_element_type=F32).astype(BF)
    for i in range(SIDE):
        grad_out[i] = grad_agg[i * ROWS : (i + 1) * ROWS, :]

    def c_copy(other, q):
        return pltpu.make_async_remote_copy(
            src_ref=grad_out.at[other],
            dst_ref=gath.at[y * 2 * SIDE + h * 2 + q],
            send_sem=c_send.at[other * 2 + q],
            recv_sem=c_recv.at[h * 2 + q],
            device_id=(y * SIDE + namer[q], other),
            device_id_type=MESH,
        )

    for other in range(SIDE):
        for q in range(2):
            here = jnp.logical_and(is_self[q], other == feat)

            @pl.when(here)
            def _(other=other, q=q):
                gath[y * 2 * SIDE + h * 2 + q] = grad_out[other]

            @pl.when(jnp.logical_not(here))
            def _(other=other, q=q):
                c_copy(other, q).start()

    grad_w = lax.dot_general(aggregated, grad_pre, NT, preferred_element_type=F32)
    grad_b = lax.dot_general(jnp.ones((ROWS, BLOCK), BF), grad_pre, NT, preferred_element_type=F32)
    upper = lax.broadcasted_iota(jnp.int32, (ROWS, BLOCK), 0) < 8
    grad_b = jnp.where(upper, grad_b[:, :BLOCK], grad_b[:, BLOCK:]).astype(BF)
    grad_w = grad_w.astype(BF)
    for i in range(SIDE):
        for half in range(2):
            at = slice(half * BLOCK, (half + 1) * BLOCK)
            terms[i, half * ROWS : (half + 1) * ROWS, :] = grad_w[i * ROWS : (i + 1) * ROWS, at]
        terms[i, 2 * ROWS :, :] = grad_b

    def r_copy(stage, step, src, dst, device):
        return pltpu.make_async_remote_copy(
            src_ref=src,
            dst_ref=dst,
            send_sem=r_send.at[stage, step],
            recv_sem=r_recv.at[stage, step],
            device_id=device,
            device_id_type=MESH,
        )

    def r_y(step):
        return r_copy(0, step, terms.at[y_peer[step]], red_y.at[y], y_device[step])

    def r_xc(step):
        return r_copy(1, step, red_xc.at[place_xc], red_xc.at[place_xc], xc_device[step])

    def r_z(step):
        return r_copy(2, step, red_z.at[place_z], red_z.at[place_z], z_device[step])

    def r_all(step):
        return r_copy(3, step, whole.at[y], whole.at[y], y_device[step])

    def r_start(make):
        for step in STEPS:
            make(step).start()

    def r_wait(stage, buffer, peer, device):
        for step in range(1, SIDE):
            r_copy(stage, step, buffer.at[0], buffer.at[peer[SIDE - step]], device[1]).wait_recv()

    def r_sent(make):
        for step in range(1, SIDE):
            make(step).wait_send()

    r_start(r_y)

    def c_wait(other, q):
        @pl.when(jnp.logical_not(jnp.logical_and(is_self[q], other == h)))
        def _():
            pltpu.make_async_remote_copy(
                src_ref=grad_out.at[0],
                dst_ref=gath.at[y * 2 * SIDE + other * 2 + q],
                send_sem=c_send.at[0],
                recv_sem=c_recv.at[other * 2 + q],
                device_id=(y * SIDE + other, holder[q]),
                device_id_type=MESH,
            ).wait_recv()

    def d_copy(turn, step):
        own = gath.at[pl.ds(y * 2 * SIDE + (z + turn) % 4 * 4, 4)]
        return pltpu.make_async_remote_copy(
            src_ref=own,
            dst_ref=own,
            send_sem=d_send.at[turn, step],
            recv_sem=d_recv.at[turn, step],
            device_id=y_device[step],
            device_id_type=MESH,
        )

    def total_of(buffer):
        total = buffer[0].astype(F32)
        for i in range(1, SIDE):
            total = total + buffer[i].astype(F32)
        return total

    for turn in NEAR_FIRST[:2]:
        for k in range(4):
            c_wait((z + turn) % 4 * 2 + k // 2, k % 2)
        for step in STEPS:
            d_copy(turn, step).start()

    red_y[y] = terms[y]
    r_wait(0, red_y, y_peer, y_device)
    red_xc[place_xc] = total_of(red_y).astype(BF)
    r_start(r_xc)
    for turn in NEAR_FIRST[2:]:
        for k in range(4):
            c_wait((z + turn) % 4 * 2 + k // 2, k % 2)
        for step in STEPS:
            d_copy(turn, step).start()

    core_copy.wait_send()
    for step in range(1, SIDE):
        a_copy(0, step).wait_send()
        a_copy(1, step).wait_send()
    r_sent(r_y)
    r_wait(1, red_xc, xc_peer, xc_device)
    red_z[place_z] = total_of(red_xc).astype(BF)
    r_start(r_z)
    for part_of in b_parts:

        @pl.when(jnp.logical_not(b_here(part_of)))
        def _(part_of=part_of):
            b_copy(part_of).wait_send()

    for other in range(SIDE):
        for q in range(2):

            @pl.when(jnp.logical_not(jnp.logical_and(is_self[q], other == feat)))
            def _(other=other, q=q):
                c_copy(other, q).wait_send()

    r_sent(r_xc)
    r_wait(2, red_z, z_peer, z_device)
    final = total_of(red_z)
    for half in range(2):
        at = slice(half * BLOCK, (half + 1) * BLOCK)
        whole[y, :, at] = final[half * ROWS : (half + 1) * ROWS, :]
        gb_ref[:, at] = final[2 * ROWS + 8 * half : 2 * ROWS + 8 * half + 1, :]
    r_start(r_all)

    for turn in NEAR_FIRST:
        for step in range(1, SIDE):
            pltpu.make_async_remote_copy(
                src_ref=gath.at[pl.ds(0, 4)],
                dst_ref=gath.at[pl.ds(y_peer[SIDE - step] * 2 * SIDE + (z + turn) % 4 * 4, 4)],
                send_sem=d_send.at[turn, step],
                recv_sem=d_recv.at[turn, step],
                device_id=y_device[1],
                device_id_type=MESH,
            ).wait_recv()

    def one_run(run, total):
        first = run * RUN
        wide = []
        for step in range(RUN):
            slot = first + step
            piece = gath[pair_of(rows_ref[0, slot], col)]
            where = jnp.where(slot < count, cols_ref[0, slot], -1)
            wide.append(
                jnp.concatenate(
                    [jnp.where(where == b, piece, jnp.zeros_like(piece)) for b in range(SIDE)], axis=0
                )
            )
        left = jnp.concatenate(wide, axis=1)
        right = vals[pl.ds(first, RUN)].reshape(RUN * BLOCK, BLOCK)
        return total + jnp.dot(left, right, preferred_element_type=F32)

    sums = lax.fori_loop(0, SLOTS // RUN, one_run, jnp.zeros((SIDE * ROWS, BLOCK), F32)).astype(BF)
    out = jnp.zeros((ROWS, NODES), F32)
    for block in range(SIDE):
        out = out + lax.dot_general(
            sums[block * ROWS : (block + 1) * ROWS, :],
            hot[:, block * BLOCK : (block + 1) * BLOCK],
            NT,
            preferred_element_type=F32,
        )
    gf_ref[...] = out.astype(BF)

    for turn in range(4):
        for step in range(1, SIDE):
            d_copy(turn, step).wait_send()
    r_sent(r_z)
    r_wait(3, whole, y_peer, y_device)
    gw_ref[...] = whole[...]
    r_sent(r_all)


def write_kernel(*refs):
    sources, targets, sems = refs[:4], refs[4:8], refs[8]
    copies = [
        pltpu.make_async_copy(source, target, sems.at[i])
        for i, (source, target) in enumerate(zip(sources, targets))
    ]
    for copy in copies:
        copy.start()
    for copy in copies:
        copy.wait()


def per_device(
    features_t,
    node_order,
    tile_rows,
    tile_cols,
    tile_vals,
    tile_count,
    weight,
    bias_term,
    cotangent,
):
    vmem = pl.BlockSpec(memory_space=pltpu.VMEM)
    hbm = pl.BlockSpec(memory_space=pl.ANY)
    operands = (
        tile_rows,
        tile_cols,
        tile_count,
        node_order.reshape(1, NODES),
        features_t,
        tile_vals.reshape(SLOTS, BLOCK, BLOCK),
        weight,
        bias_term.reshape(1, HID),
        cotangent,
    )
    operands = [
        pltpu.with_memory_space_constraint(operand, pltpu.HBM) if operand.size > 1 else operand
        for operand in operands
    ]
    dma = pltpu.SemaphoreType.DMA
    shapes = (((HID, BLOCK), BF), ((SIDE, ROWS, HID), F32), ((1, HID), F32), ((ROWS, NODES), BF))
    made = pl.pallas_call(
        exchange_kernel,
        out_shape=tuple(pltpu.VMEM(*shape) for shape in shapes),
        in_specs=[hbm] * 9,
        out_specs=(vmem,) * 4,
        scratch_shapes=[
            pltpu.SMEM((1, SLOTS), jnp.int32),
            pltpu.SMEM((1, SLOTS), jnp.int32),
            pltpu.SMEM((1,), jnp.int32),
            pltpu.VMEM((1, SLOTS), jnp.int32),
            pltpu.VMEM((1, NODES), jnp.int32),
            pltpu.VMEM((ROWS, NODES), BF),
            pltpu.VMEM((SLOTS, BLOCK, BLOCK), BF),
            pltpu.VMEM((F_IN, HID), BF),
            pltpu.VMEM((1, HID), F32),
            pltpu.VMEM((HID, BLOCK), BF),
            pltpu.VMEM((NODES, NODES), BF),
            pltpu.VMEM((SIDE, ROWS, BLOCK), BF),
            pltpu.VMEM((SLOTS * ROWS, BLOCK), F32),
            pltpu.VMEM((PAIRS * ROWS, BLOCK), F32),
            pltpu.VMEM((SIDE, 2 * SIDE, ROWS, BLOCK), BF),
            pltpu.VMEM((SIDE, 4, ROWS, BLOCK), BF),
            pltpu.VMEM((SIDE, MINE, ROWS, BLOCK), BF),
            pltpu.VMEM((MINE, ROWS, BLOCK), BF),
            pltpu.VMEM((2 * SIDE, ROWS, BLOCK), BF),
            pltpu.VMEM((F_IN, BLOCK), BF),
            pltpu.VMEM((SIDE, ROWS, BLOCK), BF),
            pltpu.VMEM((PAIRS, ROWS, BLOCK), BF),
            pltpu.VMEM((SIDE, 3 * ROWS, BLOCK), BF),
            pltpu.VMEM((SIDE, 3 * ROWS, BLOCK), BF),
            pltpu.VMEM((SIDE, 3 * ROWS, BLOCK), BF),
            pltpu.VMEM((SIDE, 3 * ROWS, BLOCK), BF),
            pltpu.VMEM((SIDE, ROWS, HID), F32),
            dma((9,)),
            dma((SLOTS // RUN,)),
            dma,
            dma,
            dma((2, SIDE)),
            dma((2, SIDE)),
            dma((MINE,)),
            dma((2 * SIDE,)),
            dma((2 * SIDE,)),
            dma((2 * SIDE,)),
            dma((4, SIDE)),
            dma((4, SIDE)),
            dma((4, SIDE)),
            dma((4, SIDE)),
        ],
        compiler_params=pltpu.CompilerParams(
            collective_id=0, has_side_effects=True, vmem_limit_bytes=VMEM_BYTES
        ),
        name="exchange_layer",
    )(*operands)
    act, grad_w, grad_b, grad_f = pl.pallas_call(
        write_kernel,
        out_shape=tuple(jax.ShapeDtypeStruct(*shape) for shape in shapes),
        in_specs=[vmem] * 4,
        out_specs=(hbm,) * 4,
        scratch_shapes=[dma((4,))],
        compiler_params=pltpu.CompilerParams(vmem_limit_bytes=4 << 20),
        name="write_outputs",
    )(*made)
    return act, grad_w.reshape(F_IN, HID), grad_b.reshape(HID), grad_f


def solution(mesh):
    return jax.shard_map(
        per_device,
        mesh=mesh,
        in_specs=(
            P("feat", "col"),
            P("col"),
            P("col", None),
            P("col", None),
            P("col", None, None, None),
            P("col"),
            P(),
            P(),
            P(None, ("col", "feat")),
        ),
        out_specs=(P(None, ("col", "feat")), P(), P(), P("feat", "col")),
        check_vma=False,
    )
```

```python
import jax
import jax.numpy as jnp
from jax import lax
from jax.experimental import pallas as pl
from jax.experimental.pallas import tpu as pltpu
from jax.sharding import PartitionSpec as P

BF = jnp.bfloat16
F32 = jnp.float32
MESH = pl.DeviceIdType.MESH
NT = (((1,), (1,)), ((), ()))

BLOCK = 128
ROWS = 16
SLOTS = 96
RUN = 12
SIDE = 8
PAIRS = 128
HID = 256
F_IN = 128
NODES = 1024
VMEM_BYTES = 40 << 20
STEPS = (4, 3, 5, 2, 6, 1, 7)
MINE = 12
NEAR_FIRST = (0, 1, 3, 2)


def pair_of(row, group):
    return (row >> 3) * 2 + jnp.minimum((row - group) & 7, 1)


def one_hot(order_row):
    node = lax.broadcasted_iota(jnp.int32, (NODES, order_row.shape[1]), 0)
    return jnp.where(node == order_row, 1.0, 0.0).astype(BF)


def exchange_kernel(
    rows_hbm,
    cols_hbm,
    count_hbm,
    order_hbm,
    feats_hbm,
    vals_hbm,
    weight_hbm,
    bias_hbm,
    cot_hbm,
    act_ref,
    gw_ref,
    gb_ref,
    gf_ref,
    rows_ref,
    cols_ref,
    count_ref,
    rows_wide,
    order_ref,
    feats_ref,
    vals,
    weight_ref,
    bias_ref,
    cot_ref,
    hot,
    perm,
    products,
    totals,
    part,
    core_in,
    from_y,
    sum_y,
    pieces,
    agg,
    grad_out,
    gath,
    terms,
    red_y,
    red_xc,
    red_z,
    whole,
    in_sem,
    vals_sem,
    core_send,
    core_recv,
    a_send,
    a_recv,
    b_send,
    b_recv,
    c_send,
    c_recv,
    d_send,
    d_recv,
    r_send,
    r_recv,
):
    col = lax.axis_index("col")
    feat = lax.axis_index("feat")
    y = col // SIDE
    h = col % SIDE
    z = h // 2

    def vals_copy(run):
        at = pl.ds(run * RUN, RUN)
        return pltpu.make_async_copy(vals_hbm.at[at], vals.at[at], vals_sem.at[run])

    inputs = [
        pltpu.make_async_copy(src, dst, in_sem.at[i])
        for i, (src, dst) in enumerate(
            (
                (order_hbm, order_ref),
                (feats_hbm, feats_ref),
                (rows_hbm, rows_ref),
                (cols_hbm, cols_ref),
                (rows_hbm, rows_wide),
                (count_hbm, count_ref),
                (weight_hbm, weight_ref),
                (bias_hbm, bias_ref),
                (cot_hbm, cot_ref),
            )
        )
    ]
    for copy in inputs[:6]:
        copy.start()
    for run in range(SLOTS // RUN):
        vals_copy(run).start()
    for copy in inputs[6:]:
        copy.start()

    x, z_lo, core = feat // 2, feat % 2, h % 2
    place_xc, place_z = x * 2 + core, z * 2 + z_lo
    y_peer, y_device, xc_peer, xc_device, z_peer, z_device = ([None] for _ in range(6))
    for step in range(1, SIDE):
        y_peer.append(lax.rem(y + step, SIDE))
        y_device.append((y_peer[step] * SIDE + h, feat))
        place = lax.rem(place_xc + step, SIDE)
        xc_peer.append(place)
        xc_device.append((y * SIDE + z * 2 + place % 2, place // 2 * 2 + z_lo))
        place = lax.rem(place_z + step, SIDE)
        z_peer.append(place)
        z_device.append((y * SIDE + place // 2 * 2 + core, x * 2 + place % 2))
    holder = (h, lax.rem(h + 1, SIDE))
    namer = (feat, lax.rem(feat + SIDE - 1, SIDE))
    is_self = (feat == holder[0], feat == holder[1])

    barrier = pltpu.get_barrier_semaphore()

    def greet(device):
        pl.semaphore_signal(barrier, inc=1, device_id=device, device_id_type=MESH)

    for other in range(SIDE):
        for q in range(2):

            @pl.when(jnp.logical_not(jnp.logical_and(is_self[q], other == h)))
            def _(other=other, q=q):
                greet((y * SIDE + other, holder[q]))

            @pl.when(jnp.logical_not(jnp.logical_and(is_self[q], other == feat)))
            def _(other=other, q=q):
                greet((y * SIDE + namer[q], other))

    for step in STEPS:
        greet(z_device[step])
        greet(y_device[step])
        greet(xc_device[step])

    inputs[0].wait()
    inputs[1].wait()
    order = order_ref[...] - col * NODES
    feats = feats_ref[...]
    for block in range(SIDE):
        at = slice(block * BLOCK, (block + 1) * BLOCK)
        hot[:, at] = one_hot(order[:, at])
        perm[block] = jnp.dot(feats, hot[:, at], preferred_element_type=F32).astype(BF)

    for copy in inputs[2:6]:
        copy.wait()
    count = count_ref[0]

    def one_forward(run, _):
        vals_copy(run).wait()
        for step in range(RUN):
            slot = run * RUN + step
            products[pl.ds(pl.multiple_of(slot * ROWS, ROWS), ROWS), :] = lax.dot_general(
                perm[cols_ref[0, slot]], vals[slot], NT, preferred_element_type=F32
            )
        return 0

    lax.fori_loop(0, SLOTS // RUN, one_forward, 0)
    row_block = rows_wide[...]
    owner_h = (row_block >> 3) & 7
    second = jnp.minimum((row_block - col) & 7, 1)
    theirs = jnp.where((owner_h & 1) == core, 0, 4)
    place = jnp.where(second == core, owner_h, 8 + (owner_h >> 1) + theirs)
    place = (row_block >> 6) * 2 * SIDE + place
    place = jnp.where(lax.broadcasted_iota(jnp.int32, (1, SLOTS), 1) < count, place, -1)
    pick = jnp.where(lax.broadcasted_iota(jnp.int32, (PAIRS, SLOTS), 0) == place, 1.0, 0.0).astype(BF)
    for f in range(ROWS):
        value = products[pl.ds(f, SLOTS, stride=ROWS), :]
        high = value.astype(BF)
        low = (value - high.astype(F32)).astype(BF)
        totals[pl.ds(f, PAIRS, stride=ROWS), :] = jnp.dot(
            pick, high, preferred_element_type=F32
        ) + jnp.dot(pick, low, preferred_element_type=F32)
    part[...] = totals[...].reshape(SIDE, 2 * SIDE, ROWS, BLOCK).astype(BF)

    for copy in inputs[6:]:
        copy.wait()
    weight = weight_ref[...]
    weight_t = weight.T
    bias = jnp.broadcast_to(bias_ref[...], (8, HID)).T[:, :1]

    selves = jnp.where(is_self[0], 1, 0) + jnp.where(is_self[1], 1, 0)
    pl.semaphore_wait(barrier, 3 * (SIDE - 1) + 4 * SIDE - 2 * selves)

    core_copy = pltpu.make_async_remote_copy(
        src_ref=part.at[:, pl.ds(MINE, 4)],
        dst_ref=core_in,
        send_sem=core_send,
        recv_sem=core_recv,
        device_id=(y * SIDE + z * 2 + 1 - core, feat),
        device_id_type=MESH,
    )
    core_copy.start()

    def a_copy(which, step):
        at = pl.ds(0, SIDE) if which == 0 else pl.ds(SIDE, 4)
        return pltpu.make_async_remote_copy(
            src_ref=part.at[y_peer[step], at],
            dst_ref=from_y.at[step, at],
            send_sem=a_send.at[which, step],
            recv_sem=a_recv.at[which, step],
            device_id=y_device[step],
            device_id_type=MESH,
        )

    for step in STEPS:
        a_copy(0, step).start()
    core_copy.wait_recv()
    for i in range(SIDE):
        at = (i * 2 * SIDE + SIDE) * ROWS
        own = totals[at : at + 4 * ROWS, :].reshape(4, ROWS, BLOCK)
        part[i, SIDE:MINE] = (own + core_in[i].astype(F32)).astype(BF)
    for step in STEPS:
        a_copy(1, step).start()

    own_block = jnp.where(core == 0, holder[0], holder[1])
    shared_block = z * 2 + 1
    far_first = [lax.rem(z + turn, 4) for turn in (2, 1, 3, 0)]
    b_own = [(i * 2 + k, i * 2 + k, own_block, core * SIDE + feat) for i in far_first for k in range(2)]
    b_shared = [(SIDE + i, i * 2 + core, shared_block, feat) for i in far_first]
    b_parts = b_own + b_shared

    def b_here(part_of):
        return jnp.logical_and(part_of[1] == h, part_of[2] == feat)

    def b_copy(part_of):
        i, other, block, slot = part_of
        return pltpu.make_async_remote_copy(
            src_ref=sum_y.at[i],
            dst_ref=pieces.at[slot],
            send_sem=b_send.at[i],
            recv_sem=b_recv.at[slot],
            device_id=(y * SIDE + other, block),
            device_id_type=MESH,
        )

    for which, parts_of in enumerate((b_own, b_shared)):
        for step in range(1, SIDE):
            a_copy(which, step).wait_recv()
        for part_of in parts_of:
            i = part_of[0]
            total = part[y, i].astype(F32)
            for step in range(1, SIDE):
                total = total + from_y[step, i].astype(F32)
            sum_y[i] = total.astype(BF)

            @pl.when(b_here(part_of))
            def _(part_of=part_of):
                pieces[part_of[3]] = sum_y[part_of[0]]

            @pl.when(jnp.logical_not(b_here(part_of)))
            def _(part_of=part_of):
                b_copy(part_of).start()

    even = feat % 2 == 0
    first_from = jnp.where(even, feat, feat - 1 + core)

    def b_wait(slot, source_h, source_feat):
        @pl.when(jnp.logical_not(jnp.logical_and(source_h == h, source_feat == feat)))
        def _():
            pltpu.make_async_remote_copy(
                src_ref=sum_y.at[0],
                dst_ref=pieces.at[slot],
                send_sem=b_send.at[0],
                recv_sem=b_recv.at[slot],
                device_id=(y * SIDE + source_h, source_feat),
                device_id_type=MESH,
            ).wait_recv()

    for source in range(SIDE):
        b_wait(source, first_from, source)

    @pl.when(even)
    def _():
        for source in range(SIDE):
            b_wait(SIDE + source, namer[1], source)

    @pl.when(jnp.logical_not(even))
    def _():
        pieces[SIDE:] = jnp.zeros((SIDE, ROWS, BLOCK), BF)

    for i in range(SIDE):
        both = pieces[i].astype(F32) + pieces[SIDE + i].astype(F32)
        agg[i * ROWS : (i + 1) * ROWS, :] = both.astype(BF)

    aggregated = agg[...]
    pre = jnp.dot(weight_t, aggregated, preferred_element_type=F32) + bias
    root = 0.7978845608028654
    square = pre * pre
    bend = jnp.tanh(root * (pre + 0.044715 * (square * pre)))
    half = 0.5 * (1.0 + bend)
    act_ref[...] = (pre * half).astype(BF)
    slope = half + 0.5 * pre * (1.0 - bend * bend) * (root * (1.0 + 3.0 * 0.044715 * square))
    grad_pre = (cot_ref[...].astype(F32) * slope).astype(BF)
    grad_agg = jnp.dot(weight, grad_pre, preferred_element_type=F32).astype(BF)
    for i in range(SIDE):
        grad_out[i] = grad_agg[i * ROWS : (i + 1) * ROWS, :]

    def c_copy(other, q):
        return pltpu.make_async_remote_copy(
            src_ref=grad_out.at[other],
            dst_ref=gath.at[y * 2 * SIDE + h * 2 + q],
            send_sem=c_send.at[other * 2 + q],
            recv_sem=c_recv.at[h * 2 + q],
            device_id=(y * SIDE + namer[q], other),
            device_id_type=MESH,
        )

    grad_w = lax.dot_general(aggregated, grad_pre, NT, preferred_element_type=F32)
    grad_b = lax.dot_general(jnp.ones((ROWS, BLOCK), BF), grad_pre, NT, preferred_element_type=F32)
    upper = lax.broadcasted_iota(jnp.int32, (ROWS, BLOCK), 0) < 8
    grad_b = jnp.where(upper, grad_b[:, :BLOCK], grad_b[:, BLOCK:]).astype(BF)
    grad_w = grad_w.astype(BF)
    for i in range(SIDE):
        for half in range(2):
            at = slice(half * BLOCK, (half + 1) * BLOCK)
            terms[i, half * ROWS : (half + 1) * ROWS, :] = grad_w[i * ROWS : (i + 1) * ROWS, at]
        terms[i, 2 * ROWS :, :] = grad_b

    def r_copy(stage, step, src, dst, device):
        return pltpu.make_async_remote_copy(
            src_ref=src,
            dst_ref=dst,
            send_sem=r_send.at[stage, step],
            recv_sem=r_recv.at[stage, step],
            device_id=device,
            device_id_type=MESH,
        )

    def r_y(step):
        return r_copy(0, step, terms.at[y_peer[step]], red_y.at[y], y_device[step])

    def r_xc(step):
        return r_copy(1, step, red_xc.at[place_xc], red_xc.at[place_xc], xc_device[step])

    def r_z(step):
        return r_copy(2, step, red_z.at[place_z], red_z.at[place_z], z_device[step])

    def r_all(step):
        return r_copy(3, step, whole.at[y], whole.at[y], y_device[step])

    def r_start(make):
        for step in STEPS:
            make(step).start()

    def r_wait(stage, buffer, peer, device):
        for step in range(1, SIDE):
            r_copy(stage, step, buffer.at[0], buffer.at[peer[SIDE - step]], device[1]).wait_recv()

    def r_sent(make):
        for step in range(1, SIDE):
            make(step).wait_send()

    r_start(r_y)

    for other in range(SIDE):
        for q in range(2):
            here = jnp.logical_and(is_self[q], other == feat)

            @pl.when(here)
            def _(other=other, q=q):
                gath[y * 2 * SIDE + h * 2 + q] = grad_out[other]

            @pl.when(jnp.logical_not(here))
            def _(other=other, q=q):
                c_copy(other, q).start()


    def c_wait(other, q):
        @pl.when(jnp.logical_not(jnp.logical_and(is_self[q], other == h)))
        def _():
            pltpu.make_async_remote_copy(
                src_ref=grad_out.at[0],
                dst_ref=gath.at[y * 2 * SIDE + other * 2 + q],
                send_sem=c_send.at[0],
                recv_sem=c_recv.at[other * 2 + q],
                device_id=(y * SIDE + other, holder[q]),
                device_id_type=MESH,
            ).wait_recv()

    def d_copy(turn, step):
        own = gath.at[pl.ds(y * 2 * SIDE + (z + turn) % 4 * 4, 4)]
        return pltpu.make_async_remote_copy(
            src_ref=own,
            dst_ref=own,
            send_sem=d_send.at[turn, step],
            recv_sem=d_recv.at[turn, step],
            device_id=y_device[step],
            device_id_type=MESH,
        )

    def total_of(buffer):
        total = buffer[0].astype(F32)
        for i in range(1, SIDE):
            total = total + buffer[i].astype(F32)
        return total

    for turn in NEAR_FIRST[:2]:
        for k in range(4):
            c_wait((z + turn) % 4 * 2 + k // 2, k % 2)
        for step in STEPS:
            d_copy(turn, step).start()

    red_y[y] = terms[y]
    r_wait(0, red_y, y_peer, y_device)
    red_xc[place_xc] = total_of(red_y).astype(BF)
    r_start(r_xc)
    for turn in NEAR_FIRST[2:]:
        for k in range(4):
            c_wait((z + turn) % 4 * 2 + k // 2, k % 2)
        for step in STEPS:
            d_copy(turn, step).start()

    core_copy.wait_send()
    for step in range(1, SIDE):
        a_copy(0, step).wait_send()
        a_copy(1, step).wait_send()
    r_sent(r_y)
    r_wait(1, red_xc, xc_peer, xc_device)
    red_z[place_z] = total_of(red_xc).astype(BF)
    r_start(r_z)
    for part_of in b_parts:

        @pl.when(jnp.logical_not(b_here(part_of)))
        def _(part_of=part_of):
            b_copy(part_of).wait_send()

    for other in range(SIDE):
        for q in range(2):

            @pl.when(jnp.logical_not(jnp.logical_and(is_self[q], other == feat)))
            def _(other=other, q=q):
                c_copy(other, q).wait_send()

    r_sent(r_xc)
    r_wait(2, red_z, z_peer, z_device)
    final = total_of(red_z)
    for half in range(2):
        at = slice(half * BLOCK, (half + 1) * BLOCK)
        whole[y, :, at] = final[half * ROWS : (half + 1) * ROWS, :]
        gb_ref[:, at] = final[2 * ROWS + 8 * half : 2 * ROWS + 8 * half + 1, :]
    r_start(r_all)

    for turn in NEAR_FIRST:
        for step in range(1, SIDE):
            pltpu.make_async_remote_copy(
                src_ref=gath.at[pl.ds(0, 4)],
                dst_ref=gath.at[pl.ds(y_peer[SIDE - step] * 2 * SIDE + (z + turn) % 4 * 4, 4)],
                send_sem=d_send.at[turn, step],
                recv_sem=d_recv.at[turn, step],
                device_id=y_device[1],
                device_id_type=MESH,
            ).wait_recv()

    def one_run(run, total):
        first = run * RUN
        wide = []
        for step in range(RUN):
            slot = first + step
            piece = gath[pair_of(rows_ref[0, slot], col)]
            where = jnp.where(slot < count, cols_ref[0, slot], -1)
            wide.append(
                jnp.concatenate(
                    [jnp.where(where == b, piece, jnp.zeros_like(piece)) for b in range(SIDE)], axis=0
                )
            )
        left = jnp.concatenate(wide, axis=1)
        right = vals[pl.ds(first, RUN)].reshape(RUN * BLOCK, BLOCK)
        return total + jnp.dot(left, right, preferred_element_type=F32)

    sums = lax.fori_loop(0, SLOTS // RUN, one_run, jnp.zeros((SIDE * ROWS, BLOCK), F32)).astype(BF)
    out = jnp.zeros((ROWS, NODES), F32)
    for block in range(SIDE):
        out = out + lax.dot_general(
            sums[block * ROWS : (block + 1) * ROWS, :],
            hot[:, block * BLOCK : (block + 1) * BLOCK],
            NT,
            preferred_element_type=F32,
        )
    gf_ref[...] = out.astype(BF)

    for turn in range(4):
        for step in range(1, SIDE):
            d_copy(turn, step).wait_send()
    r_sent(r_z)
    r_wait(3, whole, y_peer, y_device)
    gw_ref[...] = whole[...]
    r_sent(r_all)


def write_kernel(*refs):
    sources, targets, sems = refs[:4], refs[4:8], refs[8]
    copies = [
        pltpu.make_async_copy(source, target, sems.at[i])
        for i, (source, target) in enumerate(zip(sources, targets))
    ]
    for copy in copies:
        copy.start()
    for copy in copies:
        copy.wait()


def per_device(
    features_t,
    node_order,
    tile_rows,
    tile_cols,
    tile_vals,
    tile_count,
    weight,
    bias_term,
    cotangent,
):
    vmem = pl.BlockSpec(memory_space=pltpu.VMEM)
    hbm = pl.BlockSpec(memory_space=pl.ANY)
    operands = (
        tile_rows,
        tile_cols,
        tile_count,
        node_order.reshape(1, NODES),
        features_t,
        tile_vals.reshape(SLOTS, BLOCK, BLOCK),
        weight,
        bias_term.reshape(1, HID),
        cotangent,
    )
    operands = [
        pltpu.with_memory_space_constraint(operand, pltpu.HBM) if operand.size > 1 else operand
        for operand in operands
    ]
    dma = pltpu.SemaphoreType.DMA
    shapes = (((HID, BLOCK), BF), ((SIDE, ROWS, HID), F32), ((1, HID), F32), ((ROWS, NODES), BF))
    made = pl.pallas_call(
        exchange_kernel,
        out_shape=tuple(pltpu.VMEM(*shape) for shape in shapes),
        in_specs=[hbm] * 9,
        out_specs=(vmem,) * 4,
        scratch_shapes=[
            pltpu.SMEM((1, SLOTS), jnp.int32),
            pltpu.SMEM((1, SLOTS), jnp.int32),
            pltpu.SMEM((1,), jnp.int32),
            pltpu.VMEM((1, SLOTS), jnp.int32),
            pltpu.VMEM((1, NODES), jnp.int32),
            pltpu.VMEM((ROWS, NODES), BF),
            pltpu.VMEM((SLOTS, BLOCK, BLOCK), BF),
            pltpu.VMEM((F_IN, HID), BF),
            pltpu.VMEM((1, HID), F32),
            pltpu.VMEM((HID, BLOCK), BF),
            pltpu.VMEM((NODES, NODES), BF),
            pltpu.VMEM((SIDE, ROWS, BLOCK), BF),
            pltpu.VMEM((SLOTS * ROWS, BLOCK), F32),
            pltpu.VMEM((PAIRS * ROWS, BLOCK), F32),
            pltpu.VMEM((SIDE, 2 * SIDE, ROWS, BLOCK), BF),
            pltpu.VMEM((SIDE, 4, ROWS, BLOCK), BF),
            pltpu.VMEM((SIDE, MINE, ROWS, BLOCK), BF),
            pltpu.VMEM((MINE, ROWS, BLOCK), BF),
            pltpu.VMEM((2 * SIDE, ROWS, BLOCK), BF),
            pltpu.VMEM((F_IN, BLOCK), BF),
            pltpu.VMEM((SIDE, ROWS, BLOCK), BF),
            pltpu.VMEM((PAIRS, ROWS, BLOCK), BF),
            pltpu.VMEM((SIDE, 3 * ROWS, BLOCK), BF),
            pltpu.VMEM((SIDE, 3 * ROWS, BLOCK), BF),
            pltpu.VMEM((SIDE, 3 * ROWS, BLOCK), BF),
            pltpu.VMEM((SIDE, 3 * ROWS, BLOCK), BF),
            pltpu.VMEM((SIDE, ROWS, HID), F32),
            dma((9,)),
            dma((SLOTS // RUN,)),
            dma,
            dma,
            dma((2, SIDE)),
            dma((2, SIDE)),
            dma((MINE,)),
            dma((2 * SIDE,)),
            dma((2 * SIDE,)),
            dma((2 * SIDE,)),
            dma((4, SIDE)),
            dma((4, SIDE)),
            dma((4, SIDE)),
            dma((4, SIDE)),
        ],
        compiler_params=pltpu.CompilerParams(
            collective_id=0, has_side_effects=True, vmem_limit_bytes=VMEM_BYTES
        ),
        name="exchange_layer",
    )(*operands)
    act, grad_w, grad_b, grad_f = pl.pallas_call(
        write_kernel,
        out_shape=tuple(jax.ShapeDtypeStruct(*shape) for shape in shapes),
        in_specs=[vmem] * 4,
        out_specs=(hbm,) * 4,
        scratch_shapes=[dma((4,))],
        compiler_params=pltpu.CompilerParams(vmem_limit_bytes=4 << 20),
        name="write_outputs",
    )(*made)
    return act, grad_w.reshape(F_IN, HID), grad_b.reshape(HID), grad_f


def solution(mesh):
    return jax.shard_map(
        per_device,
        mesh=mesh,
        in_specs=(
            P("feat", "col"),
            P("col"),
            P("col", None),
            P("col", None),
            P("col", None, None, None),
            P("col"),
            P(),
            P(),
            P(None, ("col", "feat")),
        ),
        out_specs=(P(None, ("col", "feat")), P(), P(), P("feat", "col")),
        check_vma=False,
    )
```

```python
import jax
import jax.numpy as jnp
from jax import lax
from jax.experimental import pallas as pl
from jax.experimental.pallas import tpu as pltpu
from jax.sharding import PartitionSpec as P

BF = jnp.bfloat16
F32 = jnp.float32
MESH = pl.DeviceIdType.MESH
NT = (((1,), (1,)), ((), ()))

BLOCK = 128
ROWS = 16
SLOTS = 96
RUN = 12
SIDE = 8
PAIRS = 128
HID = 256
F_IN = 128
NODES = 1024
VMEM_BYTES = 40 << 20
STEPS = (4, 3, 5, 2, 6, 1, 7)
MINE = 12
NEAR_FIRST = (0, 1, 3, 2)


def pair_of(row, group):
    return (row >> 3) * 2 + jnp.minimum((row - group) & 7, 1)


def one_hot(order_row):
    node = lax.broadcasted_iota(jnp.int32, (NODES, order_row.shape[1]), 0)
    return jnp.where(node == order_row, 1.0, 0.0).astype(BF)


def exchange_kernel(
    rows_hbm,
    cols_hbm,
    count_hbm,
    order_hbm,
    feats_hbm,
    vals_hbm,
    weight_hbm,
    bias_hbm,
    cot_hbm,
    act_ref,
    gw_ref,
    gb_ref,
    gf_ref,
    rows_ref,
    cols_ref,
    count_ref,
    rows_wide,
    order_ref,
    feats_ref,
    vals,
    weight_ref,
    bias_ref,
    cot_ref,
    hot,
    perm,
    products,
    totals,
    part,
    core_in,
    from_y,
    sum_y,
    pieces,
    agg,
    grad_out,
    gath,
    terms,
    red_y,
    red_xc,
    red_z,
    whole,
    in_sem,
    vals_sem,
    core_send,
    core_recv,
    a_send,
    a_recv,
    b_send,
    b_recv,
    c_send,
    c_recv,
    d_send,
    d_recv,
    r_send,
    r_recv,
):
    col = lax.axis_index("col")
    feat = lax.axis_index("feat")
    y = col // SIDE
    h = col % SIDE
    z = h // 2

    def vals_copy(run):
        at = pl.ds(run * RUN, RUN)
        return pltpu.make_async_copy(vals_hbm.at[at], vals.at[at], vals_sem.at[run])

    inputs = [
        pltpu.make_async_copy(src, dst, in_sem.at[i])
        for i, (src, dst) in enumerate(
            (
                (order_hbm, order_ref),
                (feats_hbm, feats_ref),
                (rows_hbm, rows_ref),
                (cols_hbm, cols_ref),
                (rows_hbm, rows_wide),
                (count_hbm, count_ref),
                (weight_hbm, weight_ref),
                (bias_hbm, bias_ref),
                (cot_hbm, cot_ref),
            )
        )
    ]
    for copy in inputs[:6]:
        copy.start()
    for run in range(SLOTS // RUN):
        vals_copy(run).start()
    for copy in inputs[6:]:
        copy.start()

    x, z_lo, core = feat // 2, feat % 2, h % 2
    place_xc, place_z = x * 2 + core, z * 2 + z_lo
    y_peer, y_device, xc_peer, xc_device, z_peer, z_device = ([None] for _ in range(6))
    for step in range(1, SIDE):
        y_peer.append(lax.rem(y + step, SIDE))
        y_device.append((y_peer[step] * SIDE + h, feat))
        place = lax.rem(place_xc + step, SIDE)
        xc_peer.append(place)
        xc_device.append((y * SIDE + z * 2 + place % 2, place // 2 * 2 + z_lo))
        place = lax.rem(place_z + step, SIDE)
        z_peer.append(place)
        z_device.append((y * SIDE + place // 2 * 2 + core, x * 2 + place % 2))
    holder = (h, lax.rem(h + 1, SIDE))
    namer = (feat, lax.rem(feat + SIDE - 1, SIDE))
    is_self = (feat == holder[0], feat == holder[1])

    barrier = pltpu.get_barrier_semaphore()

    def greet(device):
        pl.semaphore_signal(barrier, inc=1, device_id=device, device_id_type=MESH)

    for other in range(SIDE):
        for q in range(2):

            @pl.when(jnp.logical_not(jnp.logical_and(is_self[q], other == h)))
            def _(other=other, q=q):
                greet((y * SIDE + other, holder[q]))

            @pl.when(jnp.logical_not(jnp.logical_and(is_self[q], other == feat)))
            def _(other=other, q=q):
                greet((y * SIDE + namer[q], other))

    for step in STEPS:
        greet(z_device[step])
        greet(y_device[step])
        greet(xc_device[step])

    inputs[0].wait()
    inputs[1].wait()
    order = order_ref[...] - col * NODES
    feats = feats_ref[...]
    for block in range(SIDE):
        at = slice(block * BLOCK, (block + 1) * BLOCK)
        hot[:, at] = one_hot(order[:, at])
        perm[block] = jnp.dot(feats, hot[:, at], preferred_element_type=F32).astype(BF)

    for copy in inputs[2:6]:
        copy.wait()
    count = count_ref[0]

    def one_forward(run, _):
        vals_copy(run).wait()
        for step in range(RUN):
            slot = run * RUN + step
            products[pl.ds(pl.multiple_of(slot * ROWS, ROWS), ROWS), :] = lax.dot_general(
                perm[cols_ref[0, slot]], vals[slot], NT, preferred_element_type=F32
            )
        return 0

    lax.fori_loop(0, SLOTS // RUN, one_forward, 0)
    row_block = rows_wide[...]
    owner_h = (row_block >> 3) & 7
    second = jnp.minimum((row_block - col) & 7, 1)
    theirs = jnp.where((owner_h & 1) == core, 0, 4)
    place = jnp.where(second == core, owner_h, 8 + (owner_h >> 1) + theirs)
    place = (row_block >> 6) * 2 * SIDE + place
    place = jnp.where(lax.broadcasted_iota(jnp.int32, (1, SLOTS), 1) < count, place, -1)
    pick = jnp.where(lax.broadcasted_iota(jnp.int32, (PAIRS, SLOTS), 0) == place, 1.0, 0.0).astype(BF)
    for f in range(ROWS):
        value = products[pl.ds(f, SLOTS, stride=ROWS), :]
        high = value.astype(BF)
        low = (value - high.astype(F32)).astype(BF)
        totals[pl.ds(f, PAIRS, stride=ROWS), :] = jnp.dot(
            pick, high, preferred_element_type=F32
        ) + jnp.dot(pick, low, preferred_element_type=F32)
    part[...] = totals[...].reshape(SIDE, 2 * SIDE, ROWS, BLOCK).astype(BF)

    for copy in inputs[6:]:
        copy.wait()
    weight = weight_ref[...]
    weight_t = weight.T
    bias = jnp.broadcast_to(bias_ref[...], (8, HID)).T[:, :1]

    selves = jnp.where(is_self[0], 1, 0) + jnp.where(is_self[1], 1, 0)
    pl.semaphore_wait(barrier, 3 * (SIDE - 1) + 4 * SIDE - 2 * selves)

    core_copy = pltpu.make_async_remote_copy(
        src_ref=part.at[:, pl.ds(MINE, 4)],
        dst_ref=core_in,
        send_sem=core_send,
        recv_sem=core_recv,
        device_id=(y * SIDE + z * 2 + 1 - core, feat),
        device_id_type=MESH,
    )
    core_copy.start()

    def a_copy(which, step):
        at = pl.ds(0, SIDE) if which == 0 else pl.ds(SIDE, 4)
        return pltpu.make_async_remote_copy(
            src_ref=part.at[y_peer[step], at],
            dst_ref=from_y.at[step, at],
            send_sem=a_send.at[which, step],
            recv_sem=a_recv.at[which, step],
            device_id=y_device[step],
            device_id_type=MESH,
        )

    for step in STEPS:
        a_copy(0, step).start()
    core_copy.wait_recv()
    for i in range(SIDE):
        at = (i * 2 * SIDE + SIDE) * ROWS
        own = totals[at : at + 4 * ROWS, :].reshape(4, ROWS, BLOCK)
        part[i, SIDE:MINE] = (own + core_in[i].astype(F32)).astype(BF)
    for step in STEPS:
        a_copy(1, step).start()

    own_block = jnp.where(core == 0, holder[0], holder[1])
    shared_block = z * 2 + 1
    far_first = [lax.rem(z + turn, 4) for turn in (2, 1, 3, 0)]
    b_own = [(i * 2 + k, i * 2 + k, own_block, core * SIDE + feat) for i in far_first for k in range(2)]
    b_shared = [(SIDE + i, i * 2 + core, shared_block, feat) for i in far_first]
    b_parts = b_own + b_shared

    def b_here(part_of):
        return jnp.logical_and(part_of[1] == h, part_of[2] == feat)

    def b_copy(part_of):
        i, other, block, slot = part_of
        return pltpu.make_async_remote_copy(
            src_ref=sum_y.at[i],
            dst_ref=pieces.at[slot],
            send_sem=b_send.at[i],
            recv_sem=b_recv.at[slot],
            device_id=(y * SIDE + other, block),
            device_id_type=MESH,
        )

    for which, parts_of in enumerate((b_own, b_shared)):
        for step in range(1, SIDE):
            a_copy(which, step).wait_recv()
        for part_of in parts_of:
            i = part_of[0]
            total = part[y, i].astype(F32)
            for step in range(1, SIDE):
                total = total + from_y[step, i].astype(F32)
            sum_y[i] = total.astype(BF)

            @pl.when(b_here(part_of))
            def _(part_of=part_of):
                pieces[part_of[3]] = sum_y[part_of[0]]

            @pl.when(jnp.logical_not(b_here(part_of)))
            def _(part_of=part_of):
                b_copy(part_of).start()

    even = feat % 2 == 0
    first_from = jnp.where(even, feat, feat - 1 + core)

    def b_wait(slot, source_h, source_feat):
        @pl.when(jnp.logical_not(jnp.logical_and(source_h == h, source_feat == feat)))
        def _():
            pltpu.make_async_remote_copy(
                src_ref=sum_y.at[0],
                dst_ref=pieces.at[slot],
                send_sem=b_send.at[0],
                recv_sem=b_recv.at[slot],
                device_id=(y * SIDE + source_h, source_feat),
                device_id_type=MESH,
            ).wait_recv()

    for source in range(SIDE):
        b_wait(source, first_from, source)

    @pl.when(even)
    def _():
        for source in range(SIDE):
            b_wait(SIDE + source, namer[1], source)

    @pl.when(jnp.logical_not(even))
    def _():
        pieces[SIDE:] = jnp.zeros((SIDE, ROWS, BLOCK), BF)

    for i in range(SIDE):
        both = pieces[i].astype(F32) + pieces[SIDE + i].astype(F32)
        agg[i * ROWS : (i + 1) * ROWS, :] = both.astype(BF)

    aggregated = agg[...]
    pre = jnp.dot(weight_t, aggregated, preferred_element_type=F32) + bias
    root = 0.7978845608028654
    square = pre * pre
    bend = jnp.tanh(root * (pre + 0.044715 * (square * pre)))
    half = 0.5 * (1.0 + bend)
    act_ref[...] = (pre * half).astype(BF)
    slope = half + 0.5 * pre * (1.0 - bend * bend) * (root * (1.0 + 3.0 * 0.044715 * square))
    grad_pre = (cot_ref[...].astype(F32) * slope).astype(BF)
    def c_copy(other, q):
        return pltpu.make_async_remote_copy(
            src_ref=grad_out.at[other],
            dst_ref=gath.at[y * 2 * SIDE + h * 2 + q],
            send_sem=c_send.at[other * 2 + q],
            recv_sem=c_recv.at[h * 2 + q],
            device_id=(y * SIDE + namer[q], other),
            device_id_type=MESH,
        )

    grad_w = lax.dot_general(aggregated, grad_pre, NT, preferred_element_type=F32)
    grad_b = lax.dot_general(jnp.ones((ROWS, BLOCK), BF), grad_pre, NT, preferred_element_type=F32)
    upper = lax.broadcasted_iota(jnp.int32, (ROWS, BLOCK), 0) < 8
    grad_b = jnp.where(upper, grad_b[:, :BLOCK], grad_b[:, BLOCK:]).astype(BF)
    grad_w = grad_w.astype(BF)
    for i in range(SIDE):
        for half in range(2):
            at = slice(half * BLOCK, (half + 1) * BLOCK)
            terms[i, half * ROWS : (half + 1) * ROWS, :] = grad_w[i * ROWS : (i + 1) * ROWS, at]
        terms[i, 2 * ROWS :, :] = grad_b

    def r_copy(stage, step, src, dst, device):
        return pltpu.make_async_remote_copy(
            src_ref=src,
            dst_ref=dst,
            send_sem=r_send.at[stage, step],
            recv_sem=r_recv.at[stage, step],
            device_id=device,
            device_id_type=MESH,
        )

    def r_y(step):
        return r_copy(0, step, terms.at[y_peer[step]], red_y.at[y], y_device[step])

    def r_xc(step):
        return r_copy(1, step, red_xc.at[place_xc], red_xc.at[place_xc], xc_device[step])

    def r_z(step):
        return r_copy(2, step, red_z.at[place_z], red_z.at[place_z], z_device[step])

    def r_all(step):
        return r_copy(3, step, whole.at[y], whole.at[y], y_device[step])

    def r_start(make):
        for step in STEPS:
            make(step).start()

    def r_wait(stage, buffer, peer, device):
        for step in range(1, SIDE):
            r_copy(stage, step, buffer.at[0], buffer.at[peer[SIDE - step]], device[1]).wait_recv()

    def r_sent(make):
        for step in range(1, SIDE):
            make(step).wait_send()

    r_start(r_y)

    grad_agg = jnp.dot(weight, grad_pre, preferred_element_type=F32).astype(BF)
    for i in range(SIDE):
        grad_out[i] = grad_agg[i * ROWS : (i + 1) * ROWS, :]

    for other in range(SIDE):
        for q in range(2):
            here = jnp.logical_and(is_self[q], other == feat)

            @pl.when(here)
            def _(other=other, q=q):
                gath[y * 2 * SIDE + h * 2 + q] = grad_out[other]

            @pl.when(jnp.logical_not(here))
            def _(other=other, q=q):
                c_copy(other, q).start()


    def c_wait(other, q):
        @pl.when(jnp.logical_not(jnp.logical_and(is_self[q], other == h)))
        def _():
            pltpu.make_async_remote_copy(
                src_ref=grad_out.at[0],
                dst_ref=gath.at[y * 2 * SIDE + other * 2 + q],
                send_sem=c_send.at[0],
                recv_sem=c_recv.at[other * 2 + q],
                device_id=(y * SIDE + other, holder[q]),
                device_id_type=MESH,
            ).wait_recv()

    def d_copy(turn, step):
        own = gath.at[pl.ds(y * 2 * SIDE + (z + turn) % 4 * 4, 4)]
        return pltpu.make_async_remote_copy(
            src_ref=own,
            dst_ref=own,
            send_sem=d_send.at[turn, step],
            recv_sem=d_recv.at[turn, step],
            device_id=y_device[step],
            device_id_type=MESH,
        )

    def total_of(buffer):
        total = buffer[0].astype(F32)
        for i in range(1, SIDE):
            total = total + buffer[i].astype(F32)
        return total

    for turn in NEAR_FIRST[:2]:
        for k in range(4):
            c_wait((z + turn) % 4 * 2 + k // 2, k % 2)
        for step in STEPS:
            d_copy(turn, step).start()

    red_y[y] = terms[y]
    r_wait(0, red_y, y_peer, y_device)
    red_xc[place_xc] = total_of(red_y).astype(BF)
    r_start(r_xc)
    for turn in NEAR_FIRST[2:]:
        for k in range(4):
            c_wait((z + turn) % 4 * 2 + k // 2, k % 2)
        for step in STEPS:
            d_copy(turn, step).start()

    core_copy.wait_send()
    for step in range(1, SIDE):
        a_copy(0, step).wait_send()
        a_copy(1, step).wait_send()
    r_sent(r_y)
    r_wait(1, red_xc, xc_peer, xc_device)
    red_z[place_z] = total_of(red_xc).astype(BF)
    r_start(r_z)
    for part_of in b_parts:

        @pl.when(jnp.logical_not(b_here(part_of)))
        def _(part_of=part_of):
            b_copy(part_of).wait_send()

    for other in range(SIDE):
        for q in range(2):

            @pl.when(jnp.logical_not(jnp.logical_and(is_self[q], other == feat)))
            def _(other=other, q=q):
                c_copy(other, q).wait_send()

    r_sent(r_xc)
    r_wait(2, red_z, z_peer, z_device)
    final = total_of(red_z)
    for half in range(2):
        at = slice(half * BLOCK, (half + 1) * BLOCK)
        whole[y, :, at] = final[half * ROWS : (half + 1) * ROWS, :]
        gb_ref[:, at] = final[2 * ROWS + 8 * half : 2 * ROWS + 8 * half + 1, :]
    r_start(r_all)

    for turn in NEAR_FIRST:
        for step in range(1, SIDE):
            pltpu.make_async_remote_copy(
                src_ref=gath.at[pl.ds(0, 4)],
                dst_ref=gath.at[pl.ds(y_peer[SIDE - step] * 2 * SIDE + (z + turn) % 4 * 4, 4)],
                send_sem=d_send.at[turn, step],
                recv_sem=d_recv.at[turn, step],
                device_id=y_device[1],
                device_id_type=MESH,
            ).wait_recv()

    def one_run(run, total):
        first = run * RUN
        wide = []
        for step in range(RUN):
            slot = first + step
            piece = gath[pair_of(rows_ref[0, slot], col)]
            where = jnp.where(slot < count, cols_ref[0, slot], -1)
            wide.append(
                jnp.concatenate(
                    [jnp.where(where == b, piece, jnp.zeros_like(piece)) for b in range(SIDE)], axis=0
                )
            )
        left = jnp.concatenate(wide, axis=1)
        right = vals[pl.ds(first, RUN)].reshape(RUN * BLOCK, BLOCK)
        return total + jnp.dot(left, right, preferred_element_type=F32)

    sums = lax.fori_loop(0, SLOTS // RUN, one_run, jnp.zeros((SIDE * ROWS, BLOCK), F32)).astype(BF)
    out = jnp.zeros((ROWS, NODES), F32)
    for block in range(SIDE):
        out = out + lax.dot_general(
            sums[block * ROWS : (block + 1) * ROWS, :],
            hot[:, block * BLOCK : (block + 1) * BLOCK],
            NT,
            preferred_element_type=F32,
        )
    gf_ref[...] = out.astype(BF)

    for turn in range(4):
        for step in range(1, SIDE):
            d_copy(turn, step).wait_send()
    r_sent(r_z)
    r_wait(3, whole, y_peer, y_device)
    gw_ref[...] = whole[...]
    r_sent(r_all)


def write_kernel(*refs):
    sources, targets, sems = refs[:4], refs[4:8], refs[8]
    copies = [
        pltpu.make_async_copy(source, target, sems.at[i])
        for i, (source, target) in enumerate(zip(sources, targets))
    ]
    for copy in copies:
        copy.start()
    for copy in copies:
        copy.wait()


def per_device(
    features_t,
    node_order,
    tile_rows,
    tile_cols,
    tile_vals,
    tile_count,
    weight,
    bias_term,
    cotangent,
):
    vmem = pl.BlockSpec(memory_space=pltpu.VMEM)
    hbm = pl.BlockSpec(memory_space=pl.ANY)
    operands = (
        tile_rows,
        tile_cols,
        tile_count,
        node_order.reshape(1, NODES),
        features_t,
        tile_vals.reshape(SLOTS, BLOCK, BLOCK),
        weight,
        bias_term.reshape(1, HID),
        cotangent,
    )
    operands = [
        pltpu.with_memory_space_constraint(operand, pltpu.HBM) if operand.size > 1 else operand
        for operand in operands
    ]
    dma = pltpu.SemaphoreType.DMA
    shapes = (((HID, BLOCK), BF), ((SIDE, ROWS, HID), F32), ((1, HID), F32), ((ROWS, NODES), BF))
    made = pl.pallas_call(
        exchange_kernel,
        out_shape=tuple(pltpu.VMEM(*shape) for shape in shapes),
        in_specs=[hbm] * 9,
        out_specs=(vmem,) * 4,
        scratch_shapes=[
            pltpu.SMEM((1, SLOTS), jnp.int32),
            pltpu.SMEM((1, SLOTS), jnp.int32),
            pltpu.SMEM((1,), jnp.int32),
            pltpu.VMEM((1, SLOTS), jnp.int32),
            pltpu.VMEM((1, NODES), jnp.int32),
            pltpu.VMEM((ROWS, NODES), BF),
            pltpu.VMEM((SLOTS, BLOCK, BLOCK), BF),
            pltpu.VMEM((F_IN, HID), BF),
            pltpu.VMEM((1, HID), F32),
            pltpu.VMEM((HID, BLOCK), BF),
            pltpu.VMEM((NODES, NODES), BF),
            pltpu.VMEM((SIDE, ROWS, BLOCK), BF),
            pltpu.VMEM((SLOTS * ROWS, BLOCK), F32),
            pltpu.VMEM((PAIRS * ROWS, BLOCK), F32),
            pltpu.VMEM((SIDE, 2 * SIDE, ROWS, BLOCK), BF),
            pltpu.VMEM((SIDE, 4, ROWS, BLOCK), BF),
            pltpu.VMEM((SIDE, MINE, ROWS, BLOCK), BF),
            pltpu.VMEM((MINE, ROWS, BLOCK), BF),
            pltpu.VMEM((2 * SIDE, ROWS, BLOCK), BF),
            pltpu.VMEM((F_IN, BLOCK), BF),
            pltpu.VMEM((SIDE, ROWS, BLOCK), BF),
            pltpu.VMEM((PAIRS, ROWS, BLOCK), BF),
            pltpu.VMEM((SIDE, 3 * ROWS, BLOCK), BF),
            pltpu.VMEM((SIDE, 3 * ROWS, BLOCK), BF),
            pltpu.VMEM((SIDE, 3 * ROWS, BLOCK), BF),
            pltpu.VMEM((SIDE, 3 * ROWS, BLOCK), BF),
            pltpu.VMEM((SIDE, ROWS, HID), F32),
            dma((9,)),
            dma((SLOTS // RUN,)),
            dma,
            dma,
            dma((2, SIDE)),
            dma((2, SIDE)),
            dma((MINE,)),
            dma((2 * SIDE,)),
            dma((2 * SIDE,)),
            dma((2 * SIDE,)),
            dma((4, SIDE)),
            dma((4, SIDE)),
            dma((4, SIDE)),
            dma((4, SIDE)),
        ],
        compiler_params=pltpu.CompilerParams(
            collective_id=0, has_side_effects=True, vmem_limit_bytes=VMEM_BYTES
        ),
        name="exchange_layer",
    )(*operands)
    act, grad_w, grad_b, grad_f = pl.pallas_call(
        write_kernel,
        out_shape=tuple(jax.ShapeDtypeStruct(*shape) for shape in shapes),
        in_specs=[vmem] * 4,
        out_specs=(hbm,) * 4,
        scratch_shapes=[dma((4,))],
        compiler_params=pltpu.CompilerParams(vmem_limit_bytes=4 << 20),
        name="write_outputs",
    )(*made)
    return act, grad_w.reshape(F_IN, HID), grad_b.reshape(HID), grad_f


def solution(mesh):
    return jax.shard_map(
        per_device,
        mesh=mesh,
        in_specs=(
            P("feat", "col"),
            P("col"),
            P("col", None),
            P("col", None),
            P("col", None, None, None),
            P("col"),
            P(),
            P(),
            P(None, ("col", "feat")),
        ),
        out_specs=(P(None, ("col", "feat")), P(), P(), P("feat", "col")),
        check_vma=False,
    )
```
